32 devices in a mesh: ctx: 8 (over z, y), tp: 4 (over x, core).
Axes of the slice: x: 2, y: 2, z: 4, core: 2. Of those that a mesh axis runs over, the one named last changes fastest.
Arguments:
- queries: bfloat16 [512, 3584], P('ctx', 'tp'), may hold values from -6 to 6
- keys: bfloat16 [512, 512], P('ctx', 'tp'), may hold values from -5 to 5
- values: bfloat16 [512, 512], P('ctx', 'tp'), may hold values from -6 to 6
- block_table: int32 [8], replicated, may hold values from 0 to 7, each once
- residual: bfloat16 [512, 3584], P(('ctx', 'tp')), may hold values from -6 to 6
- out_weight: bfloat16 [3584, 3584], P('tp'), may hold values from -0.5 to 0.5
- norm_gain: bfloat16 [3584], replicated, may hold values from 0.099609375 to 1.8984375
- gate_logit_weight: bfloat16 [3584], replicated, may hold values from -0.09375 to 0.09375
- gate_weight: bfloat16 [3584, 20480], P(None, 'ctx'), may hold values from -0.09375 to 0.09375
- up_weight: bfloat16 [3584, 20480], P(None, 'ctx'), may hold values from -0.09375 to 0.09375
- down_weight: bfloat16 [20480, 3584], P('ctx'), may hold values from -0.0390625 to 0.0390625
Outputs:
- layer_out: bfloat16 [512, 3584], P(('ctx', 'tp'))
The draws below stay inside these ranges and needn't reach their ends.
Inputs may be any that keep to these rules, and one draw needn't show every extreme that they name: Each entry names a different pair; slot c holds blocks block_table[c] and its mirror, counted from the end of the prompt.
All inputs are finite; a program needn't handle non-finite values.
Results may differ from the reference program's by a relative error of at most 0.017.
Values may be sent and summed in bfloat16 or wider, within the bound.
A program may use at most 128 MiB of HBM per device.

```python
import math
import jax
import jax.numpy as jnp
from jax import lax

D = 3584
HEADS = 28
KV_HEADS = 4
HEAD_DIM = 128
FF = 20480
TOK_DEV = 64
SEQ = 512
N_CTX = 8


def draw_queries(key, part):
    base = jax.random.normal(jax.random.fold_in(key, 11), (SEQ, HEADS * HEAD_DIM), jnp.float32)
    base = jnp.clip(base, -4.5, 4.5)
    return base.astype(jnp.bfloat16)


def draw_keys(key, part):
    base = jax.random.normal(jax.random.fold_in(key, 12), (SEQ, KV_HEADS * HEAD_DIM), jnp.float32)
    base = jnp.clip(base, -5.0, 5.0)
    return base.astype(jnp.bfloat16)


def shard_levels(own_key, shape, pieces, low, high):
    def one(position, shards_of):
        draws = jax.random.uniform(jax.random.fold_in(jax.random.fold_in(own_key, 6), position), (shards_of,), jnp.float32, low / len(pieces), high / len(pieces))
        return jnp.repeat(jnp.exp(draws), shape[position] // shards_of).reshape((-1,) + (1,) * (len(shape) - position - 1))

    level = one(*pieces[0])
    for cut in pieces[1:]:
        level = level * one(*cut)
    return level


def normal_values(own_key, shape, spread, bound, shards=(), kind=jnp.bfloat16):
    factor_of = shard_levels(own_key, shape, shards, -0.22, 0.18) if shards else 1.0
    values = jax.random.normal(own_key, shape, jnp.float32) * spread * factor_of
    return jnp.minimum(jnp.maximum(values, -bound), bound).astype(kind)


def setup_inputs(seed: int = 0) -> dict:
    splits = jax.random.split(jax.random.key(seed), 12)
    return {
        "queries": draw_queries(jax.random.fold_in(splits[11], 71), 0),
        "keys": draw_keys(jax.random.fold_in(splits[11], 71), 0),
        "values": normal_values(splits[2], (SEQ, KV_HEADS * HEAD_DIM), 1.0, 6.0, ((0, 8), (1, 4))),
        "block_table": jax.random.permutation(splits[3], N_CTX).astype(jnp.int32),
        "residual": normal_values(splits[4], (SEQ, D), 1.0, 6.0, ((0, 32),)),
        "out_weight": normal_values(splits[5], (HEADS * HEAD_DIM, D), HEAD_DIM ** -0.5, 0.5, ((0, 4),)),
        "norm_gain": jnp.clip(1.0 + 0.18 * jax.random.normal(splits[6], (D,), jnp.float32), 0.099609375, 1.8984375).astype(jnp.bfloat16),
        "gate_logit_weight": normal_values(splits[7], (D,), D ** -0.5, 0.09375),
        "gate_weight": normal_values(splits[8], (D, FF), D ** -0.5, 0.09375, ((1, 8),)),
        "up_weight": normal_values(splits[9], (D, FF), D ** -0.5, 0.09375, ((1, 8),)),
        "down_weight": normal_values(splits[10], (FF, D), FF ** -0.5, 0.0390625, ((0, 8),)),
    }


def positions(block_table):
    rows = jnp.arange(SEQ, dtype=jnp.int32)
    owner = rows // TOK_DEV
    local = rows % TOK_DEV
    pair = block_table[owner].astype(jnp.int32)
    half = TOK_DEV // 2
    return jnp.where(local < half, pair * half + local, (2 * N_CTX - 1 - pair) * half + local - half)

def reference(queries, keys, values, block_table, residual, out_weight, norm_gain, gate_logit_weight, gate_weight, up_weight, down_weight):
    place = positions(block_table)
    group = HEADS // KV_HEADS
    scale = HEAD_DIM ** (-0.5)
    query_heads = queries.reshape(SEQ, KV_HEADS, group, HEAD_DIM).astype(jnp.float32)
    key_heads = keys.reshape(SEQ, KV_HEADS, HEAD_DIM).astype(jnp.float32)
    value_heads = values.reshape(SEQ, KV_HEADS, HEAD_DIM).astype(jnp.float32)
    rows_block = math.gcd(SEQ, 512)

    def attend_block(index):
        first = (index * rows_block).astype(jnp.int32)
        query_block = lax.dynamic_slice_in_dim(query_heads, first, rows_block, 0)
        query_place = lax.dynamic_slice_in_dim(place, first, rows_block, 0)
        score = jnp.einsum('tkgd,pkd->kgtp', query_block, key_heads) * scale
        visible = place[None, :] <= query_place[:, None]
        score = jnp.where(visible, score, -1e+30)
        top = lax.optimization_barrier(jnp.max(score, axis=-1, keepdims=True))
        weight = jnp.where(visible, jnp.exp(score - top), 0.0)
        total = lax.optimization_barrier(jnp.sum(weight, axis=-1))
        weight_bf = weight.astype(jnp.bfloat16).astype(jnp.float32)
        summed = jnp.einsum('kgtp,pkd->kgtd', weight_bf, value_heads) / total[..., None]
        summed = jnp.transpose(summed, (2, 0, 1, 3))
        return summed.astype(jnp.bfloat16).reshape(rows_block, HEADS * HEAD_DIM)
    blocks = lax.map(attend_block, jnp.arange(SEQ // rows_block, dtype=jnp.int32))
    attended_heads = blocks.reshape(SEQ, HEADS * HEAD_DIM)
    projected = jnp.dot(attended_heads, out_weight, preferred_element_type=jnp.float32)
    attended = (residual.astype(jnp.float32) + projected).astype(jnp.bfloat16)
    attended = lax.optimization_barrier(attended)
    attended_f = attended.astype(jnp.float32)
    mean_square = lax.optimization_barrier(jnp.mean(attended_f * attended_f, axis=-1, keepdims=True))
    normed = (attended_f * lax.rsqrt(mean_square + 1e-06) * norm_gain.astype(jnp.float32)).astype(jnp.bfloat16)
    gate_prob = jax.nn.sigmoid(jnp.dot(normed, gate_logit_weight, preferred_element_type=jnp.float32))
    gate_part = jnp.dot(normed, gate_weight, preferred_element_type=jnp.float32)
    up_part = jnp.dot(normed, up_weight, preferred_element_type=jnp.float32)
    hidden = (jax.nn.silu(gate_part) * up_part).astype(jnp.bfloat16)
    shared = jnp.dot(hidden, down_weight, preferred_element_type=jnp.float32)
    return (attended_f + gate_prob[:, None] * shared).astype(jnp.bfloat16)
```

```python
import functools

import jax
import jax.numpy as jnp
from jax import lax
from jax.experimental import pallas as pl
from jax.experimental.pallas import tpu as pltpu
from jax.sharding import PartitionSpec as P

HEADS = 28
KV_HEADS = 4
HEAD_DIM = 128
GROUP = HEADS // KV_HEADS
WIDTH = 512
PROJ = 1792
DOWN_SLOTS = 4
MESH = pl.DeviceIdType.MESH


def each(first, last, body):
    if last - first <= 4:
        for index in range(first, last):
            body(index)
    else:
        lax.fori_loop(first, last, lambda i, c: (body(i), c)[1], 0)


def loop(count, body):
    lax.fori_loop(0, count, lambda i, c: (body(i), c)[1], 0)


def kernel(
    ctx_count,
    tp_count,
    queries,
    keys,
    values,
    block_table,
    residual,
    out_weight,
    vectors,
    gate_weight,
    up_weight,
    down_weight,
    out,
    q_buf,
    kv_buf,
    heads_buf,
    res_buf,
    vec_buf,
    wo,
    wg,
    wu,
    wd,
    x,
    gate_acc,
    up_acc,
    hidden,
    p_send,
    p_recv,
    p_send2,
    p_recv2,
    p_sum,
    attended,
    d_send,
    d_recv,
    d_send2,
    d_recv2,
    d_sum,
    sem_q,
    sem_small,
    sem_wo,
    sem_wg,
    sem_wu,
    sem_wd,
    kv_zs,
    kv_zr,
    kv_ys,
    kv_yr,
    x_zs,
    x_zr,
    x_ys,
    x_yr,
    p_s1,
    p_r1,
    p_s2,
    p_r2,
    d_s1,
    d_r1,
    d_s2,
    d_r2,
):
    far = ctx_count // 2
    wide = tp_count // 2
    me = lax.axis_index("ctx")
    tp = lax.axis_index("tp")
    a, b = me // 2, me % 2
    e, f = tp // 2, tp % 2
    tokens = q_buf.shape[0] * q_buf.shape[1] * q_buf.shape[2]
    quarter = q_buf.shape[2]
    half = tokens // 2
    pieces = x.shape[0]
    proj_pieces = wo.shape[0]
    slots = wd.shape[0]
    width = x.shape[-1]

    def at_a(other):
        return (other * 2 + b, tp)

    beside = (a * 2 + (1 - b), tp)

    def at_e(other):
        return (me, other * 2 + f)

    core = (me, e * 2 + (1 - f))

    def q_copy(rel, i):
        row = pl.multiple_of((i * 2 + (f if rel == 0 else 1 - f)) * quarter, quarter)
        return pltpu.make_async_copy(
            queries.at[pl.ds(row, quarter), :], q_buf.at[rel, i], sem_q.at[rel, i]
        )

    def small_copies():
        return (
            pltpu.make_async_copy(keys, kv_buf.at[0, 0, a], sem_small.at[0]),
            pltpu.make_async_copy(values, kv_buf.at[1, 0, a], sem_small.at[1]),
            pltpu.make_async_copy(residual, res_buf, sem_small.at[2]),
            pltpu.make_async_copy(vectors, vec_buf, sem_small.at[3]),
        )

    def wo_copy(n):
        column = pl.multiple_of(n * wo.shape[2], 128)
        return pltpu.make_async_copy(
            out_weight.at[:, pl.ds(column, wo.shape[2])], wo.at[n], sem_wo.at[n]
        )

    def wg_copy(k):
        row = pl.multiple_of(k * width, width)
        return pltpu.make_async_copy(
            gate_weight.at[pl.ds(row, width), :], wg.at[k], sem_wg.at[k]
        )

    def wu_copy(k):
        row = pl.multiple_of(k * width, width)
        return pltpu.make_async_copy(
            up_weight.at[pl.ds(row, width), :], wu.at[k], sem_wu.at[k]
        )

    def wd_copy(n):
        column = pl.multiple_of(n * width, width)
        return pltpu.make_async_copy(
            down_weight.at[:, pl.ds(column, width)], wd.at[n % slots], sem_wd.at[n]
        )

    for copy in small_copies():
        copy.start()
    for rel in range(2):
        for i in range(wide):
            q_copy(rel, i).start()
    for n in range(proj_pieces):
        wo_copy(n).start()

    def start_pair(k):
        wg_copy(k).start()
        wu_copy(k).start()

    loop(pieces, start_pair)
    loop(slots, lambda n: wd_copy(n).start())

    barrier = pltpu.get_barrier_semaphore()

    def greet(device):
        pl.semaphore_signal(barrier, inc=1, device_id=device, device_id_type=MESH)

    greet(beside)
    greet(core)
    each(1, far, lambda i: greet(at_a(lax.rem(a + i, far))))
    each(1, wide, lambda i: greet(at_e(lax.rem(e + i, wide))))
    pl.semaphore_wait(barrier, 2 + far - 1 + wide - 1)

    def remote(src, dst, send, recv, device):
        return pltpu.make_async_remote_copy(
            src_ref=src,
            dst_ref=dst,
            send_sem=send,
            recv_sem=recv,
            device_id=device,
            device_id_type=MESH,
        )

    def kv_far(w, i):
        return remote(
            kv_buf.at[w, 0, a],
            kv_buf.at[w, 0, a],
            kv_zs.at[w, i],
            kv_zr.at[w, a],
            at_a(lax.rem(a + i, far)),
        )

    def kv_from(w, source):
        return remote(
            kv_buf.at[w, 0, source],
            kv_buf.at[w, 0, source],
            kv_zs.at[w, 0],
            kv_zr.at[w, source],
            beside,
        )

    def kv_beside(w, source):
        return remote(
            kv_buf.at[w, 0, source],
            kv_buf.at[w, 1, source],
            kv_ys.at[w, source],
            kv_yr.at[w, source],
            beside,
        )

    for w in range(2):
        small_copies()[w].wait()
        each(1, far, lambda i, w=w: kv_far(w, i).start())
        kv_beside(w, a).start()

    key_count = 2 * far * tokens
    row = lax.broadcasted_iota(jnp.int32, (1, key_count), 1)
    slot = row // tokens
    local = row % tokens

    def place_slot(c, pair):
        owner = (c % far) * 2 + lax.rem(b + c // far, 2)
        return jnp.where(slot == c, block_table[owner], pair)

    pair = lax.fori_loop(
        0, 2 * far, place_slot, jnp.zeros((1, key_count), jnp.int32)
    )
    mirror = 2 * ctx_count - 1
    key_place = jnp.where(
        local < half, pair * half + local, (mirror - pair) * half + local - half
    )
    q_row = lax.broadcasted_iota(jnp.int32, (tokens, 1), 0)
    q_block = q_row // quarter
    q_core = jnp.where(q_block < wide, f, 1 - f)
    q_local = ((q_block % wide) * 2 + q_core) * quarter + q_row % quarter
    own = block_table[me]
    q_place = jnp.where(
        q_local < half, own * half + q_local, (mirror - own) * half + q_local - half
    )
    gate_acc[...] = jnp.zeros_like(gate_acc)
    up_acc[...] = jnp.zeros_like(up_acc)

    def kv_pass(i):
        source = lax.rem(a + i, far)
        for w in range(2):
            kv_from(w, source).wait_recv()
            kv_beside(w, source).start()

    each(1, far, kv_pass)
    for rel in range(2):
        for i in range(wide):
            q_copy(rel, i).wait()

    def kv_arrived(source):
        for w in range(2):
            kv_beside(w, source).wait_recv()

    each(0, far, kv_arrived)

    visible = key_place <= q_place
    all_keys = kv_buf[0].reshape(key_count, HEAD_DIM)
    all_values = kv_buf[1].reshape(key_count, HEAD_DIM)
    for head in range(GROUP):
        lanes = slice(head * HEAD_DIM, (head + 1) * HEAD_DIM)
        q_head = q_buf[:, :, :, lanes].reshape(tokens, HEAD_DIM)
        score = lax.dot_general(
            q_head,
            all_keys,
            (((1,), (1,)), ((), ())),
            preferred_element_type=jnp.float32,
        ) * (HEAD_DIM**-0.5)
        score = jnp.where(visible, score, -1e30)
        top = jnp.max(score, axis=-1, keepdims=True)
        weight = jnp.where(visible, jnp.exp(score - top), 0.0)
        total = jnp.sum(weight, axis=-1, keepdims=True)
        added = jnp.dot(
            weight.astype(jnp.bfloat16), all_values, preferred_element_type=jnp.float32
        )
        heads_buf[:, lanes] = (added / total).astype(jnp.bfloat16)

    def p_core(n):
        return remote(p_send.at[n], p_recv.at[n], p_s1.at[n], p_r1.at[n], core)

    def p_wide(n, i):
        other = lax.rem(e + i, wide)
        return remote(
            p_send2.at[n, other],
            p_recv2.at[n, e],
            p_s2.at[n, other],
            p_r2.at[n, e],
            at_e(other),
        )

    def p_from(n, source):
        return remote(
            p_send2.at[n, source],
            p_recv2.at[n, source],
            p_s2.at[n, source],
            p_r2.at[n, source],
            at_e(source),
        )

    def p_step(n):
        wo_copy(n).wait()
        part = jnp.dot(heads_buf[...], wo[n], preferred_element_type=jnp.float32)
        part = part.reshape(2, wide, quarter, part.shape[-1])
        p_send[n] = part[1].astype(jnp.bfloat16)
        p_core(n).start()
        p_sum[n] = part[0]

    def p_on(n):
        p_core(n).wait_recv()
        summed = p_sum[n] + p_recv[n].astype(jnp.float32)
        p_sum[n] = summed
        p_send2[n] = summed.astype(jnp.bfloat16)
        each(1, wide, lambda i: p_wide(n, i).start())

    for n in range(proj_pieces):
        p_step(n)
    for n in range(proj_pieces):
        p_on(n)
    for copy in small_copies()[2:]:
        copy.wait()
    square = jnp.zeros((quarter, 1), jnp.float32)
    for n in range(proj_pieces):
        cols = slice(n * wo.shape[2], (n + 1) * wo.shape[2])
        head_sum = p_sum[n, e]
        for i in range(1, wide):
            source = lax.rem(e + i, wide)
            p_from(n, source).wait_recv()
            head_sum = head_sum + p_recv2[n, source].astype(jnp.float32)
        att = (res_buf[:, cols].astype(jnp.float32) + head_sum).astype(jnp.bfloat16)
        att = att.astype(jnp.float32)
        attended[:, cols] = att
        square = square + jnp.sum(att * att, axis=-1, keepdims=True)
    depth = proj_pieces * wo.shape[2]
    inverse = lax.rsqrt(square / depth + 1e-6)

    def x_far(k, i):
        return remote(
            x.at[k, 0, a],
            x.at[k, 0, a],
            x_zs.at[k, i],
            x_zr.at[k, a],
            at_a(lax.rem(a + i, far)),
        )

    def x_from(k, source):
        return remote(
            x.at[k, 0, source],
            x.at[k, 0, source],
            x_zs.at[k, 0],
            x_zr.at[k, source],
            beside,
        )

    def x_beside(k, source):
        return remote(
            x.at[k, 0, source],
            x.at[k, 1, source],
            x_ys.at[k, source],
            x_yr.at[k, source],
            beside,
        )

    logit = jnp.zeros((quarter, 1), jnp.float32)
    for k in range(pieces):
        cols = slice(k * width, (k + 1) * width)
        normed = (attended[:, cols] * inverse * vec_buf[0:1, cols]).astype(jnp.bfloat16)
        x[k, 0, a] = normed
        each(1, far, lambda i, k=k: x_far(k, i).start())
        x_beside(k, a).start()
        logit = logit + jnp.sum(
            normed.astype(jnp.float32) * vec_buf[1:2, cols], axis=-1, keepdims=True
        )
    gate_prob = jax.nn.sigmoid(logit)

    def x_pass(k):
        def one(i):
            source = lax.rem(a + i, far)
            x_from(k, source).wait_recv()
            x_beside(k, source).start()

        each(1, far, one)

    rows = 2 * far * quarter

    def expand(k):
        @pl.when(k + 1 < pieces)
        def _():
            x_pass(k + 1)

        wg_copy(k).wait()
        wu_copy(k).wait()
        each(0, far, lambda source: x_beside(k, source).wait_recv())
        piece = x[k].reshape(rows, width)
        gate_acc[...] += jnp.dot(piece, wg[k], preferred_element_type=jnp.float32)
        up_acc[...] += jnp.dot(piece, wu[k], preferred_element_type=jnp.float32)

    x_pass(0)
    loop(pieces, expand)
    gate = gate_acc[...]
    hidden[...] = (gate / (1.0 + jnp.exp(-gate)) * up_acc[...]).astype(jnp.bfloat16)

    def d_beside(n):
        return remote(d_send.at[n], d_recv.at[n], d_s1.at[n], d_r1.at[n], beside)

    def d_far(n, i):
        other = lax.rem(a + i, far)
        return remote(
            d_send2.at[n, other],
            d_recv2.at[n, a],
            d_s2.at[n, other],
            d_r2.at[n, a],
            at_a(other),
        )

    def d_from(n, source):
        return remote(
            d_send2.at[n, source],
            d_recv2.at[n, source],
            d_s2.at[n, source],
            d_r2.at[n, source],
            at_a(source),
        )

    def d_on(n):
        d_beside(n).wait_recv()
        summed = d_sum[n] + d_recv[n].astype(jnp.float32)
        d_sum[n] = summed
        d_send2[n] = summed.astype(jnp.bfloat16)
        each(1, far, lambda i: d_far(n, i).start())

    def contract(n):
        wd_copy(n).wait()
        part = jnp.dot(hidden[...], wd[n % slots], preferred_element_type=jnp.float32)
        part = part.reshape(2, far, quarter, width)
        d_send[n] = part[1].astype(jnp.bfloat16)
        d_beside(n).start()
        d_sum[n] = part[0]

        @pl.when(n + slots < pieces)
        def _():
            wd_copy(n + slots).start()

        @pl.when(n > 0)
        def _():
            d_on(n - 1)

    loop(pieces, contract)
    d_on(pieces - 1)
    for n in range(pieces):
        cols = slice(n * width, (n + 1) * width)
        shared = d_sum[n, a]

        def add(i, shared, n=n):
            source = lax.rem(a + i, far)
            d_from(n, source).wait_recv()
            return shared + d_recv2[n, source].astype(jnp.float32)

        if far <= 4:
            for i in range(1, far):
                shared = add(i, shared)
        else:
            shared = lax.fori_loop(1, far, add, shared)
        out[:, cols] = (attended[:, cols] + gate_prob * shared).astype(jnp.bfloat16)

    for w in range(2):
        each(1, far, lambda i, w=w: kv_far(w, i).wait_send())
        each(0, far, lambda source, w=w: kv_beside(w, source).wait_send())
    for n in range(proj_pieces):
        p_core(n).wait_send()
        each(1, wide, lambda i, n=n: p_wide(n, i).wait_send())

    def drain(k):
        each(1, far, lambda i: x_far(k, i).wait_send())
        each(0, far, lambda source: x_beside(k, source).wait_send())
        d_beside(k).wait_send()
        each(1, far, lambda i: d_far(k, i).wait_send())

    loop(pieces, drain)


def per_device(
    queries,
    keys,
    values,
    block_table,
    residual,
    out_weight,
    norm_gain,
    gate_logit_weight,
    gate_weight,
    up_weight,
    down_weight,
):
    tokens = queries.shape[0]
    ctx_count = lax.axis_size("ctx")
    tp_count = lax.axis_size("tp")
    far, wide = ctx_count // 2, tp_count // 2
    quarter, depth = residual.shape
    units = gate_weight.shape[1]
    pieces = depth // WIDTH
    proj_pieces = depth // PROJ
    slots = min(DOWN_SLOTS, pieces)
    rows = ctx_count * quarter
    vectors = jnp.stack([norm_gain, gate_logit_weight]).astype(jnp.float32)
    bf16, f32 = jnp.bfloat16, jnp.float32
    dma = pltpu.SemaphoreType.DMA
    any_space = pl.BlockSpec(memory_space=pl.ANY)
    matmul = rows * depth * units * 3 + tokens * queries.shape[1] * depth
    return pl.pallas_call(
        functools.partial(kernel, ctx_count, tp_count),
        out_shape=jax.ShapeDtypeStruct((quarter, depth), bf16),
        in_specs=[any_space] * 3
        + [pl.BlockSpec(memory_space=pltpu.SMEM)]
        + [any_space] * 6,
        out_specs=pl.BlockSpec(memory_space=pltpu.VMEM),
        scratch_shapes=[
            pltpu.VMEM((2, wide, quarter, queries.shape[1]), bf16),
            pltpu.VMEM((2, 2, far, tokens, HEAD_DIM), bf16),
            pltpu.VMEM((tokens, queries.shape[1]), bf16),
            pltpu.VMEM((quarter, depth), bf16),
            pltpu.VMEM((2, depth), f32),
            pltpu.VMEM((proj_pieces, out_weight.shape[0], PROJ), bf16),
            pltpu.VMEM((pieces, WIDTH, units), bf16),
            pltpu.VMEM((pieces, WIDTH, units), bf16),
            pltpu.VMEM((slots, units, WIDTH), bf16),
            pltpu.VMEM((pieces, 2, far, quarter, WIDTH), bf16),
            pltpu.VMEM((rows, units), f32),
            pltpu.VMEM((rows, units), f32),
            pltpu.VMEM((rows, units), bf16),
            pltpu.VMEM((proj_pieces, wide, quarter, PROJ), bf16),
            pltpu.VMEM((proj_pieces, wide, quarter, PROJ), bf16),
            pltpu.VMEM((proj_pieces, wide, quarter, PROJ), bf16),
            pltpu.VMEM((proj_pieces, wide, quarter, PROJ), bf16),
            pltpu.VMEM((proj_pieces, wide, quarter, PROJ), f32),
            pltpu.VMEM((quarter, depth), f32),
            pltpu.VMEM((pieces, far, quarter, WIDTH), bf16),
            pltpu.VMEM((pieces, far, quarter, WIDTH), bf16),
            pltpu.VMEM((pieces, far, quarter, WIDTH), bf16),
            pltpu.VMEM((pieces, far, quarter, WIDTH), bf16),
            pltpu.VMEM((pieces, far, quarter, WIDTH), f32),
            dma((2, wide)),
            dma((4,)),
            dma((proj_pieces,)),
            dma((pieces,)),
            dma((pieces,)),
            dma((pieces,)),
            dma((2, far)),
            dma((2, far)),
            dma((2, far)),
            dma((2, far)),
            dma((pieces, far)),
            dma((pieces, far)),
            dma((pieces, far)),
            dma((pieces, far)),
            dma((proj_pieces,)),
            dma((proj_pieces,)),
            dma((proj_pieces, wide)),
            dma((proj_pieces, wide)),
            dma((pieces,)),
            dma((pieces,)),
            dma((pieces, far)),
            dma((pieces, far)),
        ],
        compiler_params=pltpu.CompilerParams(
            collective_id=0,
            has_side_effects=True,
            vmem_limit_bytes=63 * 1024 * 1024,
        ),
        cost_estimate=pl.CostEstimate(
            flops=2 * matmul,
            bytes_accessed=2 * (3 * depth * units + out_weight.size),
            transcendentals=rows * units,
        ),
        name="layer",
    )(
        queries,
        keys,
        values,
        block_table,
        residual,
        out_weight,
        vectors,
        gate_weight,
        up_weight,
        down_weight,
    )


def solution(mesh):
    return jax.shard_map(
        per_device,
        mesh=mesh,
        in_specs=(
            P("ctx", "tp"),
            P("ctx", "tp"),
            P("ctx", "tp"),
            P(),
            P(("ctx", "tp"), None),
            P("tp", None),
            P(),
            P(),
            P(None, "ctx"),
            P(None, "ctx"),
            P("ctx", None),
        ),
        out_specs=P(("ctx", "tp"), None),
        check_vma=False,
    )
```

```python
import functools

import jax
import jax.numpy as jnp
from jax import lax
from jax.experimental import pallas as pl
from jax.experimental.pallas import tpu as pltpu
from jax.sharding import PartitionSpec as P

HEADS = 28
KV_HEADS = 4
HEAD_DIM = 128
GROUP = HEADS // KV_HEADS
WIDTH = 512
PROJ = 1792
DOWN_SLOTS = 4
AHEAD = 2
BEHIND = 3
MESH = pl.DeviceIdType.MESH


def each(first, last, body):
    if last - first <= 4:
        for index in range(first, last):
            body(index)
    else:
        lax.fori_loop(first, last, lambda i, c: (body(i), c)[1], 0)


def loop(count, body):
    lax.fori_loop(0, count, lambda i, c: (body(i), c)[1], 0)


def kernel(
    ctx_count,
    tp_count,
    queries,
    keys,
    values,
    block_table,
    residual,
    out_weight,
    norm_gain,
    logit_weight,
    gate_weight,
    up_weight,
    down_weight,
    out,
    q_buf,
    kv_buf,
    heads_buf,
    res_buf,
    gain_buf,
    logit_buf,
    wo,
    wg,
    wu,
    wd,
    x,
    gate_acc,
    up_acc,
    hidden,
    p_send,
    p_recv,
    p_send2,
    p_recv2,
    p_sum,
    attended,
    d_send,
    d_recv,
    d_send2,
    d_recv2,
    d_sum,
    sem_q,
    sem_small,
    sem_wo,
    sem_wg,
    sem_wu,
    sem_wd,
    kv_zs,
    kv_zr,
    kv_ys,
    kv_yr,
    x_zs,
    x_zr,
    x_ys,
    x_yr,
    p_s1,
    p_r1,
    p_s2,
    p_r2,
    d_s1,
    d_r1,
    d_s2,
    d_r2,
):
    far = ctx_count // 2
    wide = tp_count // 2
    me = lax.axis_index("ctx")
    tp = lax.axis_index("tp")
    a, b = me // 2, me % 2
    e, f = tp // 2, tp % 2
    tokens = q_buf.shape[0] * q_buf.shape[1] * q_buf.shape[2]
    quarter = q_buf.shape[2]
    half = tokens // 2
    pieces = x.shape[0]
    proj_pieces = wo.shape[0]
    slots = wd.shape[0]
    width = x.shape[-1]

    def at_a(other):
        return (other * 2 + b, tp)

    beside = (a * 2 + (1 - b), tp)

    def at_e(other):
        return (me, other * 2 + f)

    core = (me, e * 2 + (1 - f))

    def q_copy(rel, i):
        row = pl.multiple_of((i * 2 + (f if rel == 0 else 1 - f)) * quarter, quarter)
        return pltpu.make_async_copy(
            queries.at[pl.ds(row, quarter), :], q_buf.at[rel, i], sem_q.at[rel, i]
        )

    def small_copies():
        return (
            pltpu.make_async_copy(keys, kv_buf.at[0, 0, a], sem_small.at[0]),
            pltpu.make_async_copy(values, kv_buf.at[1, 0, a], sem_small.at[1]),
            pltpu.make_async_copy(residual, res_buf, sem_small.at[2]),
            pltpu.make_async_copy(norm_gain, gain_buf, sem_small.at[3]),
            pltpu.make_async_copy(logit_weight, logit_buf, sem_small.at[4]),
        )

    def wo_copy(n):
        column = pl.multiple_of(n * wo.shape[2], 128)
        return pltpu.make_async_copy(
            out_weight.at[:, pl.ds(column, wo.shape[2])], wo.at[n], sem_wo.at[n]
        )

    def wg_copy(k):
        row = pl.multiple_of(k * width, width)
        return pltpu.make_async_copy(
            gate_weight.at[pl.ds(row, width), :], wg.at[k], sem_wg.at[k]
        )

    def wu_copy(k):
        row = pl.multiple_of(k * width, width)
        return pltpu.make_async_copy(
            up_weight.at[pl.ds(row, width), :], wu.at[k], sem_wu.at[k]
        )

    def wd_copy(n):
        column = pl.multiple_of(n * width, width)
        return pltpu.make_async_copy(
            down_weight.at[:, pl.ds(column, width)], wd.at[n % slots], sem_wd.at[n]
        )

    for copy in small_copies():
        copy.start()
    for rel in range(2):
        for i in range(wide):
            q_copy(rel, i).start()
    for n in range(proj_pieces):
        wo_copy(n).start()

    def start_pair(k):
        wg_copy(k).start()
        wu_copy(k).start()

    loop(pieces, start_pair)
    loop(slots, lambda n: wd_copy(n).start())

    barrier = pltpu.get_barrier_semaphore()

    def greet(device):
        pl.semaphore_signal(barrier, inc=1, device_id=device, device_id_type=MESH)

    greet(beside)
    greet(core)
    each(1, far, lambda i: greet(at_a(lax.rem(a + i, far))))
    each(1, wide, lambda i: greet(at_e(lax.rem(e + i, wide))))
    pl.semaphore_wait(barrier, 2 + far - 1 + wide - 1)

    def remote(src, dst, send, recv, device):
        return pltpu.make_async_remote_copy(
            src_ref=src,
            dst_ref=dst,
            send_sem=send,
            recv_sem=recv,
            device_id=device,
            device_id_type=MESH,
        )

    def kv_far(w, i):
        return remote(
            kv_buf.at[w, 0, a],
            kv_buf.at[w, 0, a],
            kv_zs.at[w, i],
            kv_zr.at[w, a],
            at_a(lax.rem(a + i, far)),
        )

    def kv_from(w, source):
        return remote(
            kv_buf.at[w, 0, source],
            kv_buf.at[w, 0, source],
            kv_zs.at[w, 0],
            kv_zr.at[w, source],
            beside,
        )

    def kv_beside(w, source):
        return remote(
            kv_buf.at[w, 0, source],
            kv_buf.at[w, 1, source],
            kv_ys.at[w, source],
            kv_yr.at[w, source],
            beside,
        )

    for w in range(2):
        small_copies()[w].wait()
        each(1, far, lambda i, w=w: kv_far(w, i).start())
        kv_beside(w, a).start()

    key_count = 2 * far * tokens
    row = lax.broadcasted_iota(jnp.int32, (1, key_count), 1)
    slot = row // tokens
    local = row % tokens

    def place_slot(c, pair):
        owner = (c % far) * 2 + lax.rem(b + c // far, 2)
        return jnp.where(slot == c, block_table[owner], pair)

    pair = lax.fori_loop(
        0, 2 * far, place_slot, jnp.zeros((1, key_count), jnp.int32)
    )
    mirror = 2 * ctx_count - 1
    key_place = jnp.where(
        local < half, pair * half + local, (mirror - pair) * half + local - half
    )
    q_row = lax.broadcasted_iota(jnp.int32, (tokens, 1), 0)
    q_block = q_row // quarter
    q_core = jnp.where(q_block < wide, f, 1 - f)
    q_local = ((q_block % wide) * 2 + q_core) * quarter + q_row % quarter
    own = block_table[me]
    q_place = jnp.where(
        q_local < half, own * half + q_local, (mirror - own) * half + q_local - half
    )
    gate_acc[...] = jnp.zeros_like(gate_acc)
    up_acc[...] = jnp.zeros_like(up_acc)

    def kv_pass(i):
        source = lax.rem(a + i, far)
        for w in range(2):
            kv_from(w, source).wait_recv()
            kv_beside(w, source).start()

    each(1, far, kv_pass)
    for rel in range(2):
        for i in range(wide):
            q_copy(rel, i).wait()

    def kv_arrived(source):
        for w in range(2):
            kv_beside(w, source).wait_recv()

    each(0, far, kv_arrived)

    visible = key_place <= q_place
    all_keys = kv_buf[0].reshape(key_count, HEAD_DIM)
    all_values = kv_buf[1].reshape(key_count, HEAD_DIM)
    for head in range(GROUP):
        lanes = slice(head * HEAD_DIM, (head + 1) * HEAD_DIM)
        q_head = q_buf[:, :, :, lanes].reshape(tokens, HEAD_DIM)
        score = lax.dot_general(
            q_head,
            all_keys,
            (((1,), (1,)), ((), ())),
            preferred_element_type=jnp.float32,
        ) * (HEAD_DIM**-0.5)
        score = jnp.where(visible, score, -1e30)
        top = jnp.max(score, axis=-1, keepdims=True)
        weight = jnp.where(visible, jnp.exp(score - top), 0.0)
        total = jnp.sum(weight, axis=-1, keepdims=True)
        added = jnp.dot(
            weight.astype(jnp.bfloat16), all_values, preferred_element_type=jnp.float32
        )
        heads_buf[:, lanes] = (added / total).astype(jnp.bfloat16)

    def p_core(n):
        return remote(p_send.at[n], p_recv.at[n], p_s1.at[n], p_r1.at[n], core)

    def p_wide(n, i):
        other = lax.rem(e + i, wide)
        return remote(
            p_send2.at[n, other],
            p_recv2.at[n, e],
            p_s2.at[n, other],
            p_r2.at[n, e],
            at_e(other),
        )

    def p_from(n, source):
        return remote(
            p_send2.at[n, source],
            p_recv2.at[n, source],
            p_s2.at[n, source],
            p_r2.at[n, source],
            at_e(source),
        )

    def p_step(n):
        wo_copy(n).wait()
        part = jnp.dot(heads_buf[...], wo[n], preferred_element_type=jnp.float32)
        part = part.reshape(2, wide, quarter, part.shape[-1])
        p_send[n] = part[1].astype(jnp.bfloat16)
        p_core(n).start()
        p_sum[n] = part[0]

    def p_on(n):
        p_core(n).wait_recv()
        summed = p_sum[n] + p_recv[n].astype(jnp.float32)
        p_sum[n] = summed
        p_send2[n] = summed.astype(jnp.bfloat16)
        each(1, wide, lambda i: p_wide(n, i).start())

    for n in range(proj_pieces):
        p_step(n)
    for n in range(proj_pieces):
        p_on(n)
    for copy in small_copies()[2:]:
        copy.wait()
    square = jnp.zeros((quarter, 1), jnp.float32)
    for n in range(proj_pieces):
        cols = slice(n * wo.shape[2], (n + 1) * wo.shape[2])
        head_sum = p_sum[n, e]
        for i in range(1, wide):
            source = lax.rem(e + i, wide)
            p_from(n, source).wait_recv()
            head_sum = head_sum + p_recv2[n, source].astype(jnp.float32)
        att = (res_buf[:, cols].astype(jnp.float32) + head_sum).astype(jnp.bfloat16)
        att = att.astype(jnp.float32)
        attended[:, cols] = att
        square = square + jnp.sum(att * att, axis=-1, keepdims=True)
    depth = proj_pieces * wo.shape[2]
    inverse = lax.rsqrt(square / depth + 1e-6)

    def x_far(k, i):
        return remote(
            x.at[k, 0, a],
            x.at[k, 0, a],
            x_zs.at[k, i],
            x_zr.at[k, a],
            at_a(lax.rem(a + i, far)),
        )

    def x_from(k, source):
        return remote(
            x.at[k, 0, source],
            x.at[k, 0, source],
            x_zs.at[k, 0],
            x_zr.at[k, source],
            beside,
        )

    def x_beside(k, source):
        return remote(
            x.at[k, 0, source],
            x.at[k, 1, source],
            x_ys.at[k, source],
            x_yr.at[k, source],
            beside,
        )

    logit = jnp.zeros((quarter, 1), jnp.float32)
    for k in range(pieces):
        cols = slice(k * width, (k + 1) * width)
        normed = (attended[:, cols] * inverse * gain_buf[cols].astype(jnp.float32).reshape(1, width)).astype(jnp.bfloat16)
        x[k, 0, a] = normed
        each(1, far, lambda i, k=k: x_far(k, i).start())
        x_beside(k, a).start()
        logit = logit + jnp.sum(
            normed.astype(jnp.float32) * logit_buf[cols].astype(jnp.float32).reshape(1, width), axis=-1, keepdims=True
        )
    gate_prob = jax.nn.sigmoid(logit)

    def x_pass(k):
        def one(i):
            source = lax.rem(a + i, far)
            x_from(k, source).wait_recv()
            x_beside(k, source).start()

        each(1, far, one)

    rows = 2 * far * quarter

    def expand(k):
        @pl.when(k + AHEAD < pieces)
        def _():
            x_pass(k + AHEAD)

        wg_copy(k).wait()
        wu_copy(k).wait()
        each(0, far, lambda source: x_beside(k, source).wait_recv())
        piece = x[k].reshape(rows, width)
        gate_acc[...] += jnp.dot(piece, wg[k], preferred_element_type=jnp.float32)
        up_acc[...] += jnp.dot(piece, wu[k], preferred_element_type=jnp.float32)

    for k in range(min(AHEAD, pieces)):
        x_pass(k)
    loop(pieces, expand)
    gate = gate_acc[...]
    hidden[...] = (gate / (1.0 + jnp.exp(-gate)) * up_acc[...]).astype(jnp.bfloat16)

    def d_beside(n):
        return remote(d_send.at[n], d_recv.at[n], d_s1.at[n], d_r1.at[n], beside)

    def d_far(n, i):
        other = lax.rem(a + i, far)
        return remote(
            d_send2.at[n, other],
            d_recv2.at[n, a],
            d_s2.at[n, other],
            d_r2.at[n, a],
            at_a(other),
        )

    def d_from(n, source):
        return remote(
            d_send2.at[n, source],
            d_recv2.at[n, source],
            d_s2.at[n, source],
            d_r2.at[n, source],
            at_a(source),
        )

    def d_on(n):
        d_beside(n).wait_recv()
        summed = d_sum[n] + d_recv[n].astype(jnp.float32)
        d_sum[n] = summed
        d_send2[n] = summed.astype(jnp.bfloat16)
        each(1, far, lambda i: d_far(n, i).start())

    def contract(n):
        wd_copy(n).wait()
        part = jnp.dot(hidden[...], wd[n % slots], preferred_element_type=jnp.float32)
        part = part.reshape(2, far, quarter, width)
        d_send[n] = part[1].astype(jnp.bfloat16)
        d_beside(n).start()
        d_sum[n] = part[0]

        @pl.when(n + slots < pieces)
        def _():
            wd_copy(n + slots).start()

        @pl.when(n >= BEHIND)
        def _():
            d_on(n - BEHIND)

    loop(pieces, contract)
    for n in range(max(pieces - BEHIND, 0), pieces):
        d_on(n)
    for n in range(pieces):
        cols = slice(n * width, (n + 1) * width)
        shared = d_sum[n, a]

        def add(i, shared, n=n):
            source = lax.rem(a + i, far)
            d_from(n, source).wait_recv()
            return shared + d_recv2[n, source].astype(jnp.float32)

        if far <= 4:
            for i in range(1, far):
                shared = add(i, shared)
        else:
            shared = lax.fori_loop(1, far, add, shared)
        out[:, cols] = attended[:, cols] + gate_prob * shared

    for w in range(2):
        each(1, far, lambda i, w=w: kv_far(w, i).wait_send())
        each(0, far, lambda source, w=w: kv_beside(w, source).wait_send())
    for n in range(proj_pieces):
        p_core(n).wait_send()
        each(1, wide, lambda i, n=n: p_wide(n, i).wait_send())

    def drain(k):
        each(1, far, lambda i: x_far(k, i).wait_send())
        each(0, far, lambda source: x_beside(k, source).wait_send())
        d_beside(k).wait_send()
        each(1, far, lambda i: d_far(k, i).wait_send())

    loop(pieces, drain)


def per_device(
    queries,
    keys,
    values,
    block_table,
    residual,
    out_weight,
    norm_gain,
    gate_logit_weight,
    gate_weight,
    up_weight,
    down_weight,
):
    tokens = queries.shape[0]
    ctx_count = lax.axis_size("ctx")
    tp_count = lax.axis_size("tp")
    far, wide = ctx_count // 2, tp_count // 2
    quarter, depth = residual.shape
    units = gate_weight.shape[1]
    pieces = depth // WIDTH
    proj_pieces = depth // PROJ
    slots = min(DOWN_SLOTS, pieces)
    rows = ctx_count * quarter
    bf16, f32 = jnp.bfloat16, jnp.float32
    dma = pltpu.SemaphoreType.DMA
    any_space = pl.BlockSpec(memory_space=pl.ANY)
    matmul = rows * depth * units * 3 + tokens * queries.shape[1] * depth
    layer_out = pl.pallas_call(
        functools.partial(kernel, ctx_count, tp_count),
        out_shape=jax.ShapeDtypeStruct((quarter, depth), f32),
        in_specs=[any_space] * 3
        + [pl.BlockSpec(memory_space=pltpu.SMEM)]
        + [any_space] * 7,
        out_specs=pl.BlockSpec(memory_space=pltpu.VMEM),
        scratch_shapes=[
            pltpu.VMEM((2, wide, quarter, queries.shape[1]), bf16),
            pltpu.VMEM((2, 2, far, tokens, HEAD_DIM), bf16),
            pltpu.VMEM((tokens, queries.shape[1]), bf16),
            pltpu.VMEM((quarter, depth), bf16),
            pltpu.VMEM((depth,), bf16),
            pltpu.VMEM((depth,), bf16),
            pltpu.VMEM((proj_pieces, out_weight.shape[0], PROJ), bf16),
            pltpu.VMEM((pieces, WIDTH, units), bf16),
            pltpu.VMEM((pieces, WIDTH, units), bf16),
            pltpu.VMEM((slots, units, WIDTH), bf16),
            pltpu.VMEM((pieces, 2, far, quarter, WIDTH), bf16),
            pltpu.VMEM((rows, units), f32),
            pltpu.VMEM((rows, units), f32),
            pltpu.VMEM((rows, units), bf16),
            pltpu.VMEM((proj_pieces, wide, quarter, PROJ), bf16),
            pltpu.VMEM((proj_pieces, wide, quarter, PROJ), bf16),
            pltpu.VMEM((proj_pieces, wide, quarter, PROJ), bf16),
            pltpu.VMEM((proj_pieces, wide, quarter, PROJ), bf16),
            pltpu.VMEM((proj_pieces, wide, quarter, PROJ), f32),
            pltpu.VMEM((quarter, depth), f32),
            pltpu.VMEM((pieces, far, quarter, WIDTH), bf16),
            pltpu.VMEM((pieces, far, quarter, WIDTH), bf16),
            pltpu.VMEM((pieces, far, quarter, WIDTH), bf16),
            pltpu.VMEM((pieces, far, quarter, WIDTH), bf16),
            pltpu.VMEM((pieces, far, quarter, WIDTH), f32),
            dma((2, wide)),
            dma((5,)),
            dma((proj_pieces,)),
            dma((pieces,)),
            dma((pieces,)),
            dma((pieces,)),
            dma((2, far)),
            dma((2, far)),
            dma((2, far)),
            dma((2, far)),
            dma((pieces, far)),
            dma((pieces, far)),
            dma((pieces, far)),
            dma((pieces, far)),
            dma((proj_pieces,)),
            dma((proj_pieces,)),
            dma((proj_pieces, wide)),
            dma((proj_pieces, wide)),
            dma((pieces,)),
            dma((pieces,)),
            dma((pieces, far)),
            dma((pieces, far)),
        ],
        compiler_params=pltpu.CompilerParams(
            collective_id=0,
            has_side_effects=True,
            vmem_limit_bytes=63 * 1024 * 1024,
        ),
        cost_estimate=pl.CostEstimate(
            flops=2 * matmul,
            bytes_accessed=2 * (3 * depth * units + out_weight.size),
            transcendentals=rows * units,
        ),
        name="layer",
    )(
        queries,
        keys,
        values,
        block_table,
        residual,
        out_weight,
        norm_gain,
        gate_logit_weight,
        gate_weight,
        up_weight,
        down_weight,
    )
    return layer_out.astype(bf16)


def solution(mesh):
    return jax.shard_map(
        per_device,
        mesh=mesh,
        in_specs=(
            P("ctx", "tp"),
            P("ctx", "tp"),
            P("ctx", "tp"),
            P(),
            P(("ctx", "tp"), None),
            P("tp", None),
            P(),
            P(),
            P(None, "ctx"),
            P(None, "ctx"),
            P("ctx", None),
        ),
        out_specs=P(("ctx", "tp"), None),
        check_vma=False,
    )
```

```python
import functools

import jax
import jax.numpy as jnp
from jax import lax
from jax.experimental import pallas as pl
from jax.experimental.pallas import tpu as pltpu
from jax.sharding import PartitionSpec as P

HEADS = 28
KV_HEADS = 4
HEAD_DIM = 128
GROUP = HEADS // KV_HEADS
WIDTH = 512
PROJ = 1792
DOWN_SLOTS = 4
AHEAD = 2
BEHIND = 3
MESH = pl.DeviceIdType.MESH


def each(first, last, body):
    if last - first <= 4:
        for index in range(first, last):
            body(index)
    else:
        lax.fori_loop(first, last, lambda i, c: (body(i), c)[1], 0)


def loop(count, body):
    lax.fori_loop(0, count, lambda i, c: (body(i), c)[1], 0)


def kernel(
    ctx_count,
    tp_count,
    queries,
    keys,
    values,
    block_table,
    residual,
    out_weight,
    norm_gain,
    logit_weight,
    gate_weight,
    up_weight,
    down_weight,
    out,
    q_buf,
    kv_buf,
    heads_buf,
    res_buf,
    gain_buf,
    logit_buf,
    wo,
    wg,
    wu,
    wd,
    x,
    gate_acc,
    up_acc,
    hidden,
    p_send,
    p_recv,
    p_send2,
    p_recv2,
    p_sum,
    attended,
    d_send,
    d_recv,
    d_send2,
    d_recv2,
    d_sum,
    sem_q,
    sem_small,
    sem_wo,
    sem_wg,
    sem_wu,
    sem_wd,
    kv_zs,
    kv_zr,
    kv_ys,
    kv_yr,
    x_zs,
    x_zr,
    x_ys,
    x_yr,
    p_s1,
    p_r1,
    p_s2,
    p_r2,
    d_s1,
    d_r1,
    d_s2,
    d_r2,
):
    far = ctx_count // 2
    wide = tp_count // 2
    me = lax.axis_index("ctx")
    tp = lax.axis_index("tp")
    a, b = me // 2, me % 2
    e, f = tp // 2, tp % 2
    tokens = q_buf.shape[0] * q_buf.shape[1] * q_buf.shape[2]
    quarter = q_buf.shape[2]
    half = tokens // 2
    pieces = x.shape[0]
    proj_pieces = wo.shape[0]
    slots = wd.shape[0]
    width = x.shape[-1]

    def at_a(other):
        return (other * 2 + b, tp)

    beside = (a * 2 + (1 - b), tp)

    def at_e(other):
        return (me, other * 2 + f)

    core = (me, e * 2 + (1 - f))

    def q_copy(rel, i):
        row = pl.multiple_of((i * 2 + (f if rel == 0 else 1 - f)) * quarter, quarter)
        return pltpu.make_async_copy(
            queries.at[pl.ds(row, quarter), :], q_buf.at[rel, i], sem_q.at[rel, i]
        )

    def small_copies():
        return (
            pltpu.make_async_copy(keys, kv_buf.at[0, 0, a], sem_small.at[0]),
            pltpu.make_async_copy(values, kv_buf.at[1, 0, a], sem_small.at[1]),
            pltpu.make_async_copy(residual, res_buf, sem_small.at[2]),
            pltpu.make_async_copy(norm_gain, gain_buf, sem_small.at[3]),
            pltpu.make_async_copy(logit_weight, logit_buf, sem_small.at[4]),
        )

    def wo_copy(n):
        column = pl.multiple_of(n * wo.shape[2], 128)
        return pltpu.make_async_copy(
            out_weight.at[:, pl.ds(column, wo.shape[2])], wo.at[n], sem_wo.at[n]
        )

    def wg_copy(k):
        row = pl.multiple_of(k * width, width)
        return pltpu.make_async_copy(
            gate_weight.at[pl.ds(row, width), :], wg.at[k], sem_wg.at[k]
        )

    def wu_copy(k):
        row = pl.multiple_of(k * width, width)
        return pltpu.make_async_copy(
            up_weight.at[pl.ds(row, width), :], wu.at[k], sem_wu.at[k]
        )

    def wd_copy(n):
        column = pl.multiple_of(n * width, width)
        return pltpu.make_async_copy(
            down_weight.at[:, pl.ds(column, width)], wd.at[n % slots], sem_wd.at[n]
        )

    for copy in small_copies():
        copy.start()
    for rel in range(2):
        for i in range(wide):
            q_copy(rel, i).start()
    for n in range(proj_pieces):
        wo_copy(n).start()

    def start_pair(k):
        wg_copy(k).start()
        wu_copy(k).start()

    barrier = pltpu.get_barrier_semaphore()

    def greet(device):
        pl.semaphore_signal(barrier, inc=1, device_id=device, device_id_type=MESH)

    greet(beside)
    greet(core)
    each(1, far, lambda i: greet(at_a(lax.rem(a + i, far))))
    each(1, wide, lambda i: greet(at_e(lax.rem(e + i, wide))))
    pl.semaphore_wait(barrier, 2 + far - 1 + wide - 1)

    def remote(src, dst, send, recv, device):
        return pltpu.make_async_remote_copy(
            src_ref=src,
            dst_ref=dst,
            send_sem=send,
            recv_sem=recv,
            device_id=device,
            device_id_type=MESH,
        )

    def kv_far(w, i):
        return remote(
            kv_buf.at[w, 0, a],
            kv_buf.at[w, 0, a],
            kv_zs.at[w, i],
            kv_zr.at[w, a],
            at_a(lax.rem(a + i, far)),
        )

    def kv_from(w, source):
        return remote(
            kv_buf.at[w, 0, source],
            kv_buf.at[w, 0, source],
            kv_zs.at[w, 0],
            kv_zr.at[w, source],
            beside,
        )

    def kv_beside(w, source):
        return remote(
            kv_buf.at[w, 0, source],
            kv_buf.at[w, 1, source],
            kv_ys.at[w, source],
            kv_yr.at[w, source],
            beside,
        )

    for w in range(2):
        small_copies()[w].wait()
        each(1, far, lambda i, w=w: kv_far(w, i).start())
        kv_beside(w, a).start()
    start_pair(0)

    key_count = 2 * far * tokens
    row = lax.broadcasted_iota(jnp.int32, (1, key_count), 1)
    slot = row // tokens
    local = row % tokens

    def place_slot(c, pair):
        owner = (c % far) * 2 + lax.rem(b + c // far, 2)
        return jnp.where(slot == c, block_table[owner], pair)

    pair = lax.fori_loop(
        0, 2 * far, place_slot, jnp.zeros((1, key_count), jnp.int32)
    )
    mirror = 2 * ctx_count - 1
    key_place = jnp.where(
        local < half, pair * half + local, (mirror - pair) * half + local - half
    )
    q_row = lax.broadcasted_iota(jnp.int32, (tokens, 1), 0)
    q_block = q_row // quarter
    q_core = jnp.where(q_block < wide, f, 1 - f)
    q_local = ((q_block % wide) * 2 + q_core) * quarter + q_row % quarter
    own = block_table[me]
    q_place = jnp.where(
        q_local < half, own * half + q_local, (mirror - own) * half + q_local - half
    )
    gate_acc[...] = jnp.zeros_like(gate_acc)
    up_acc[...] = jnp.zeros_like(up_acc)

    def kv_pass(i):
        source = lax.rem(a + i, far)
        for w in range(2):
            kv_from(w, source).wait_recv()
            kv_beside(w, source).start()

    each(1, far, kv_pass)
    start_pair(1)
    start_pair(2)
    for rel in range(2):
        for i in range(wide):
            q_copy(rel, i).wait()

    def kv_arrived(source):
        for w in range(2):
            kv_beside(w, source).wait_recv()

    each(0, far, kv_arrived)

    start_pair(3)
    visible = key_place <= q_place
    all_keys = kv_buf[0].reshape(key_count, HEAD_DIM)
    all_values = kv_buf[1].reshape(key_count, HEAD_DIM)
    for head in range(GROUP):
        lanes = slice(head * HEAD_DIM, (head + 1) * HEAD_DIM)
        q_head = q_buf[:, :, :, lanes].reshape(tokens, HEAD_DIM)
        score = lax.dot_general(
            q_head,
            all_keys,
            (((1,), (1,)), ((), ())),
            preferred_element_type=jnp.float32,
        ) * (HEAD_DIM**-0.5)
        score = jnp.where(visible, score, -1e30)
        top = jnp.max(score, axis=-1, keepdims=True)
        weight = jnp.where(visible, jnp.exp(score - top), 0.0)
        total = jnp.sum(weight, axis=-1, keepdims=True)
        added = jnp.dot(
            weight.astype(jnp.bfloat16), all_values, preferred_element_type=jnp.float32
        )
        heads_buf[:, lanes] = (added / total).astype(jnp.bfloat16)

    def p_core(n):
        return remote(p_send.at[n], p_recv.at[n], p_s1.at[n], p_r1.at[n], core)

    def p_wide(n, i):
        other = lax.rem(e + i, wide)
        return remote(
            p_send2.at[n, other],
            p_recv2.at[n, e],
            p_s2.at[n, other],
            p_r2.at[n, e],
            at_e(other),
        )

    def p_from(n, source):
        return remote(
            p_send2.at[n, source],
            p_recv2.at[n, source],
            p_s2.at[n, source],
            p_r2.at[n, source],
            at_e(source),
        )

    def p_step(n):
        wo_copy(n).wait()
        part = jnp.dot(heads_buf[...], wo[n], preferred_element_type=jnp.float32)
        part = part.reshape(2, wide, quarter, part.shape[-1])
        p_send[n] = part[1].astype(jnp.bfloat16)
        p_core(n).start()
        p_sum[n] = part[0]

    def p_on(n):
        p_core(n).wait_recv()
        summed = p_sum[n] + p_recv[n].astype(jnp.float32)
        p_sum[n] = summed
        p_send2[n] = summed.astype(jnp.bfloat16)
        each(1, wide, lambda i: p_wide(n, i).start())

    for n in range(proj_pieces):
        p_step(n)
    for n in range(proj_pieces):
        p_on(n)
    start_pair(4)
    for copy in small_copies()[2:]:
        copy.wait()
    square = jnp.zeros((quarter, 1), jnp.float32)
    for n in range(proj_pieces):
        cols = slice(n * wo.shape[2], (n + 1) * wo.shape[2])
        head_sum = p_sum[n, e]
        for i in range(1, wide):
            source = lax.rem(e + i, wide)
            p_from(n, source).wait_recv()
            head_sum = head_sum + p_recv2[n, source].astype(jnp.float32)
        att = (res_buf[:, cols].astype(jnp.float32) + head_sum).astype(jnp.bfloat16)
        att = att.astype(jnp.float32)
        attended[:, cols] = att
        square = square + jnp.sum(att * att, axis=-1, keepdims=True)
    depth = proj_pieces * wo.shape[2]
    inverse = lax.rsqrt(square / depth + 1e-6)

    def x_far(k, i):
        return remote(
            x.at[k, 0, a],
            x.at[k, 0, a],
            x_zs.at[k, i],
            x_zr.at[k, a],
            at_a(lax.rem(a + i, far)),
        )

    def x_from(k, source):
        return remote(
            x.at[k, 0, source],
            x.at[k, 0, source],
            x_zs.at[k, 0],
            x_zr.at[k, source],
            beside,
        )

    def x_beside(k, source):
        return remote(
            x.at[k, 0, source],
            x.at[k, 1, source],
            x_ys.at[k, source],
            x_yr.at[k, source],
            beside,
        )

    logit = jnp.zeros((quarter, 1), jnp.float32)
    for k in range(pieces):
        cols = slice(k * width, (k + 1) * width)
        normed = (attended[:, cols] * inverse * gain_buf[cols].astype(jnp.float32).reshape(1, width)).astype(jnp.bfloat16)
        x[k, 0, a] = normed
        each(1, far, lambda i, k=k: x_far(k, i).start())
        x_beside(k, a).start()
        logit = logit + jnp.sum(
            normed.astype(jnp.float32) * logit_buf[cols].astype(jnp.float32).reshape(1, width), axis=-1, keepdims=True
        )
    gate_prob = jax.nn.sigmoid(logit)
    start_pair(5)

    def x_pass(k):
        def one(i):
            source = lax.rem(a + i, far)
            x_from(k, source).wait_recv()
            x_beside(k, source).start()

        each(1, far, one)

    rows = 2 * far * quarter

    def expand(k):
        @pl.when(k + AHEAD < pieces)
        def _():
            x_pass(k + AHEAD)

        @pl.when(k + 6 < pieces)
        def _():
            start_pair(k + 6)

        @pl.when((k >= 1) & (k <= slots))
        def _():
            wd_copy(k - 1).start()

        wg_copy(k).wait()
        wu_copy(k).wait()
        each(0, far, lambda source: x_beside(k, source).wait_recv())
        piece = x[k].reshape(rows, width)
        gate_acc[...] += jnp.dot(piece, wg[k], preferred_element_type=jnp.float32)
        up_acc[...] += jnp.dot(piece, wu[k], preferred_element_type=jnp.float32)

    for k in range(min(AHEAD, pieces)):
        x_pass(k)
    loop(pieces, expand)
    gate = gate_acc[...]
    hidden[...] = (gate / (1.0 + jnp.exp(-gate)) * up_acc[...]).astype(jnp.bfloat16)

    def d_beside(n):
        return remote(d_send.at[n], d_recv.at[n], d_s1.at[n], d_r1.at[n], beside)

    def d_far(n, i):
        other = lax.rem(a + i, far)
        return remote(
            d_send2.at[n, other],
            d_recv2.at[n, a],
            d_s2.at[n, other],
            d_r2.at[n, a],
            at_a(other),
        )

    def d_from(n, source):
        return remote(
            d_send2.at[n, source],
            d_recv2.at[n, source],
            d_s2.at[n, source],
            d_r2.at[n, source],
            at_a(source),
        )

    def d_on(n):
        d_beside(n).wait_recv()
        summed = d_sum[n] + d_recv[n].astype(jnp.float32)
        d_sum[n] = summed
        d_send2[n] = summed.astype(jnp.bfloat16)
        each(1, far, lambda i: d_far(n, i).start())

    def contract(n):
        wd_copy(n).wait()
        part = jnp.dot(hidden[...], wd[n % slots], preferred_element_type=jnp.float32)
        part = part.reshape(2, far, quarter, width)
        d_send[n] = part[1].astype(jnp.bfloat16)
        d_beside(n).start()
        d_sum[n] = part[0]

        @pl.when(n + slots < pieces)
        def _():
            wd_copy(n + slots).start()

        @pl.when(n >= BEHIND)
        def _():
            d_on(n - BEHIND)

    loop(pieces, contract)
    for n in range(max(pieces - BEHIND, 0), pieces):
        d_on(n)
    for n in range(pieces):
        cols = slice(n * width, (n + 1) * width)
        shared = d_sum[n, a]

        def add(i, shared, n=n):
            source = lax.rem(a + i, far)
            d_from(n, source).wait_recv()
            return shared + d_recv2[n, source].astype(jnp.float32)

        if far <= 4:
            for i in range(1, far):
                shared = add(i, shared)
        else:
            shared = lax.fori_loop(1, far, add, shared)
        out[:, cols] = attended[:, cols] + gate_prob * shared

    for w in range(2):
        each(1, far, lambda i, w=w: kv_far(w, i).wait_send())
        each(0, far, lambda source, w=w: kv_beside(w, source).wait_send())
    for n in range(proj_pieces):
        p_core(n).wait_send()
        each(1, wide, lambda i, n=n: p_wide(n, i).wait_send())

    def drain(k):
        each(1, far, lambda i: x_far(k, i).wait_send())
        each(0, far, lambda source: x_beside(k, source).wait_send())
        d_beside(k).wait_send()
        each(1, far, lambda i: d_far(k, i).wait_send())

    loop(pieces, drain)


def per_device(
    queries,
    keys,
    values,
    block_table,
    residual,
    out_weight,
    norm_gain,
    gate_logit_weight,
    gate_weight,
    up_weight,
    down_weight,
):
    tokens = queries.shape[0]
    ctx_count = lax.axis_size("ctx")
    tp_count = lax.axis_size("tp")
    far, wide = ctx_count // 2, tp_count // 2
    quarter, depth = residual.shape
    units = gate_weight.shape[1]
    pieces = depth // WIDTH
    proj_pieces = depth // PROJ
    slots = min(DOWN_SLOTS, pieces)
    rows = ctx_count * quarter
    bf16, f32 = jnp.bfloat16, jnp.float32
    dma = pltpu.SemaphoreType.DMA
    any_space = pl.BlockSpec(memory_space=pl.ANY)
    matmul = rows * depth * units * 3 + tokens * queries.shape[1] * depth
    layer_out = pl.pallas_call(
        functools.partial(kernel, ctx_count, tp_count),
        out_shape=jax.ShapeDtypeStruct((quarter, depth), f32),
        in_specs=[any_space] * 3
        + [pl.BlockSpec(memory_space=pltpu.SMEM)]
        + [any_space] * 7,
        out_specs=pl.BlockSpec(memory_space=pltpu.VMEM),
        scratch_shapes=[
            pltpu.VMEM((2, wide, quarter, queries.shape[1]), bf16),
            pltpu.VMEM((2, 2, far, tokens, HEAD_DIM), bf16),
            pltpu.VMEM((tokens, queries.shape[1]), bf16),
            pltpu.VMEM((quarter, depth), bf16),
            pltpu.VMEM((depth,), bf16),
            pltpu.VMEM((depth,), bf16),
            pltpu.VMEM((proj_pieces, out_weight.shape[0], PROJ), bf16),
            pltpu.VMEM((pieces, WIDTH, units), bf16),
            pltpu.VMEM((pieces, WIDTH, units), bf16),
            pltpu.VMEM((slots, units, WIDTH), bf16),
            pltpu.VMEM((pieces, 2, far, quarter, WIDTH), bf16),
            pltpu.VMEM((rows, units), f32),
            pltpu.VMEM((rows, units), f32),
            pltpu.VMEM((rows, units), bf16),
            pltpu.VMEM((proj_pieces, wide, quarter, PROJ), bf16),
            pltpu.VMEM((proj_pieces, wide, quarter, PROJ), bf16),
            pltpu.VMEM((proj_pieces, wide, quarter, PROJ), bf16),
            pltpu.VMEM((proj_pieces, wide, quarter, PROJ), bf16),
            pltpu.VMEM((proj_pieces, wide, quarter, PROJ), f32),
            pltpu.VMEM((quarter, depth), f32),
            pltpu.VMEM((pieces, far, quarter, WIDTH), bf16),
            pltpu.VMEM((pieces, far, quarter, WIDTH), bf16),
            pltpu.VMEM((pieces, far, quarter, WIDTH), bf16),
            pltpu.VMEM((pieces, far, quarter, WIDTH), bf16),
            pltpu.VMEM((pieces, far, quarter, WIDTH), f32),
            dma((2, wide)),
            dma((5,)),
            dma((proj_pieces,)),
            dma((pieces,)),
            dma((pieces,)),
            dma((pieces,)),
            dma((2, far)),
            dma((2, far)),
            dma((2, far)),
            dma((2, far)),
            dma((pieces, far)),
            dma((pieces, far)),
            dma((pieces, far)),
            dma((pieces, far)),
            dma((proj_pieces,)),
            dma((proj_pieces,)),
            dma((proj_pieces, wide)),
            dma((proj_pieces, wide)),
            dma((pieces,)),
            dma((pieces,)),
            dma((pieces, far)),
            dma((pieces, far)),
        ],
        compiler_params=pltpu.CompilerParams(
            collective_id=0,
            has_side_effects=True,
            vmem_limit_bytes=63 * 1024 * 1024,
        ),
        cost_estimate=pl.CostEstimate(
            flops=2 * matmul,
            bytes_accessed=2 * (3 * depth * units + out_weight.size),
            transcendentals=rows * units,
        ),
        name="layer",
    )(
        queries,
        keys,
        values,
        block_table,
        residual,
        out_weight,
        norm_gain,
        gate_logit_weight,
        gate_weight,
        up_weight,
        down_weight,
    )
    return layer_out.astype(bf16)


def solution(mesh):
    return jax.shard_map(
        per_device,
        mesh=mesh,
        in_specs=(
            P("ctx", "tp"),
            P("ctx", "tp"),
            P("ctx", "tp"),
            P(),
            P(("ctx", "tp"), None),
            P("tp", None),
            P(),
            P(),
            P(None, "ctx"),
            P(None, "ctx"),
            P("ctx", None),
        ),
        out_specs=P(("ctx", "tp"), None),
        check_vma=False,
    )
```

```python
import functools

import jax
import jax.numpy as jnp
from jax import lax
from jax.experimental import pallas as pl
from jax.experimental.pallas import tpu as pltpu
from jax.sharding import PartitionSpec as P

HEADS = 28
KV_HEADS = 4
HEAD_DIM = 128
GROUP = HEADS // KV_HEADS
WIDTH = 512
PROJ = WIDTH
DOWN_SLOTS = 3
AHEAD = 2
BEHIND = 3
MESH = pl.DeviceIdType.MESH


def each(first, last, body):
    if last - first <= 4:
        for index in range(first, last):
            body(index)
    else:
        lax.fori_loop(first, last, lambda i, c: (body(i), c)[1], 0)


def loop(count, body):
    lax.fori_loop(0, count, lambda i, c: (body(i), c)[1], 0)


def kernel(
    ctx_count,
    tp_count,
    queries,
    keys,
    values,
    block_table,
    residual,
    out_weight,
    norm_gain,
    logit_weight,
    gate_weight,
    up_weight,
    down_weight,
    out,
    q_buf,
    kv_buf,
    heads_buf,
    res_buf,
    gain_buf,
    logit_buf,
    wo,
    wg,
    wu,
    wd,
    x,
    gate_acc,
    up_acc,
    hidden,
    p_send,
    p_recv,
    p_send2,
    p_recv2,
    p_sum,
    attended,
    d_send,
    d_recv,
    d_send2,
    d_recv2,
    d_sum,
    sem_q,
    sem_small,
    sem_wo,
    sem_wg,
    sem_wu,
    sem_wd,
    kv_zs,
    kv_zr,
    kv_ys,
    kv_yr,
    x_zs,
    x_zr,
    x_ys,
    x_yr,
    p_s1,
    p_r1,
    p_s2,
    p_r2,
    d_s1,
    d_r1,
    d_s2,
    d_r2,
    inv_buf,
    inv_zs,
    inv_zr,
    inv_ys,
    inv_yr,
):
    far = ctx_count // 2
    wide = tp_count // 2
    me = lax.axis_index("ctx")
    tp = lax.axis_index("tp")
    a, b = me // 2, me % 2
    e, f = tp // 2, tp % 2
    tokens = q_buf.shape[0] * q_buf.shape[1] * q_buf.shape[2]
    quarter = q_buf.shape[2]
    half = tokens // 2
    pieces = x.shape[0]
    proj_pieces = wo.shape[0]
    slots = wd.shape[0]
    width = x.shape[-1]

    def at_a(other):
        return (other * 2 + b, tp)

    beside = (a * 2 + (1 - b), tp)

    def at_e(other):
        return (me, other * 2 + f)

    core = (me, e * 2 + (1 - f))

    def q_copy(rel, i):
        row = pl.multiple_of((i * 2 + (f if rel == 0 else 1 - f)) * quarter, quarter)
        return pltpu.make_async_copy(
            queries.at[pl.ds(row, quarter), :], q_buf.at[rel, i], sem_q.at[rel, i]
        )

    def small_copies():
        return (
            pltpu.make_async_copy(keys, kv_buf.at[0, 0, a], sem_small.at[0]),
            pltpu.make_async_copy(values, kv_buf.at[1, 0, a], sem_small.at[1]),
            pltpu.make_async_copy(residual, res_buf, sem_small.at[2]),
            pltpu.make_async_copy(norm_gain, gain_buf, sem_small.at[3]),
            pltpu.make_async_copy(logit_weight, logit_buf, sem_small.at[4]),
        )

    def wo_copy(n):
        column = pl.multiple_of(n * wo.shape[2], 128)
        return pltpu.make_async_copy(
            out_weight.at[:, pl.ds(column, wo.shape[2])], wo.at[n], sem_wo.at[n]
        )

    def wg_copy(k):
        row = pl.multiple_of(k * width, width)
        return pltpu.make_async_copy(
            gate_weight.at[pl.ds(row, width), :], wg.at[k], sem_wg.at[k]
        )

    def wu_copy(k):
        row = pl.multiple_of(k * width, width)
        return pltpu.make_async_copy(
            up_weight.at[pl.ds(row, width), :], wu.at[k], sem_wu.at[k]
        )

    def wd_copy(n):
        column = pl.multiple_of(n * width, width)
        return pltpu.make_async_copy(
            down_weight.at[:, pl.ds(column, width)], wd.at[n % slots], sem_wd.at[n]
        )

    for copy in small_copies():
        copy.start()
    for rel in range(2):
        for i in range(wide):
            q_copy(rel, i).start()
    for n in range(proj_pieces):
        wo_copy(n).start()

    def start_pair(k):
        wg_copy(k).start()
        wu_copy(k).start()

    barrier = pltpu.get_barrier_semaphore()

    def greet(device):
        pl.semaphore_signal(barrier, inc=1, device_id=device, device_id_type=MESH)

    greet(beside)
    greet(core)
    each(1, far, lambda i: greet(at_a(lax.rem(a + i, far))))
    each(1, wide, lambda i: greet(at_e(lax.rem(e + i, wide))))
    pl.semaphore_wait(barrier, 2 + far - 1 + wide - 1)

    def remote(src, dst, send, recv, device):
        return pltpu.make_async_remote_copy(
            src_ref=src,
            dst_ref=dst,
            send_sem=send,
            recv_sem=recv,
            device_id=device,
            device_id_type=MESH,
        )

    def kv_far(w, i):
        return remote(
            kv_buf.at[w, 0, a],
            kv_buf.at[w, 0, a],
            kv_zs.at[w, i],
            kv_zr.at[w, a],
            at_a(lax.rem(a + i, far)),
        )

    def kv_from(w, source):
        return remote(
            kv_buf.at[w, 0, source],
            kv_buf.at[w, 0, source],
            kv_zs.at[w, 0],
            kv_zr.at[w, source],
            beside,
        )

    def kv_beside(w, source):
        return remote(
            kv_buf.at[w, 0, source],
            kv_buf.at[w, 1, source],
            kv_ys.at[w, source],
            kv_yr.at[w, source],
            beside,
        )

    for w in range(2):
        small_copies()[w].wait()
        each(1, far, lambda i, w=w: kv_far(w, i).start())
        kv_beside(w, a).start()
    start_pair(0)

    key_count = 2 * far * tokens
    row = lax.broadcasted_iota(jnp.int32, (1, key_count), 1)
    slot = row // tokens
    local = row % tokens

    def place_slot(c, pair):
        owner = (c % far) * 2 + lax.rem(b + c // far, 2)
        return jnp.where(slot == c, block_table[owner], pair)

    pair = lax.fori_loop(
        0, 2 * far, place_slot, jnp.zeros((1, key_count), jnp.int32)
    )
    mirror = 2 * ctx_count - 1
    key_place = jnp.where(
        local < half, pair * half + local, (mirror - pair) * half + local - half
    )
    q_row = lax.broadcasted_iota(jnp.int32, (tokens, 1), 0)
    q_block = q_row // quarter
    q_core = jnp.where(q_block < wide, f, 1 - f)
    q_local = ((q_block % wide) * 2 + q_core) * quarter + q_row % quarter
    own = block_table[me]
    q_place = jnp.where(
        q_local < half, own * half + q_local, (mirror - own) * half + q_local - half
    )
    gate_acc[...] = jnp.zeros_like(gate_acc)
    up_acc[...] = jnp.zeros_like(up_acc)

    def kv_pass(i):
        source = lax.rem(a + i, far)
        for w in range(2):
            kv_from(w, source).wait_recv()
            kv_beside(w, source).start()

    each(1, far, kv_pass)
    start_pair(1)
    start_pair(2)
    for rel in range(2):
        for i in range(wide):
            q_copy(rel, i).wait()

    def kv_arrived(source):
        for w in range(2):
            kv_beside(w, source).wait_recv()

    each(0, far, kv_arrived)

    start_pair(3)
    visible = key_place <= q_place
    all_keys = kv_buf[0].reshape(key_count, HEAD_DIM)
    all_values = kv_buf[1].reshape(key_count, HEAD_DIM)
    for head in range(GROUP):
        lanes = slice(head * HEAD_DIM, (head + 1) * HEAD_DIM)
        q_head = q_buf[:, :, :, lanes].reshape(tokens, HEAD_DIM)
        score = lax.dot_general(
            q_head,
            all_keys,
            (((1,), (1,)), ((), ())),
            preferred_element_type=jnp.float32,
        ) * (HEAD_DIM**-0.5)
        score = jnp.where(visible, score, -1e30)
        top = jnp.max(score, axis=-1, keepdims=True)
        weight = jnp.where(visible, jnp.exp(score - top), 0.0)
        total = jnp.sum(weight, axis=-1, keepdims=True)
        added = jnp.dot(
            weight.astype(jnp.bfloat16), all_values, preferred_element_type=jnp.float32
        )
        heads_buf[:, lanes] = (added / total).astype(jnp.bfloat16)

    def p_core(n):
        return remote(p_send.at[n], p_recv.at[n], p_s1.at[n], p_r1.at[n], core)

    def p_wide(n, i):
        other = lax.rem(e + i, wide)
        return remote(
            p_send2.at[n, other],
            p_recv2.at[n, e],
            p_s2.at[n, other],
            p_r2.at[n, e],
            at_e(other),
        )

    def p_from(n, source):
        return remote(
            p_send2.at[n, source],
            p_recv2.at[n, source],
            p_s2.at[n, source],
            p_r2.at[n, source],
            at_e(source),
        )

    def p_step(n):
        wo_copy(n).wait()
        part = jnp.dot(heads_buf[...], wo[n], preferred_element_type=jnp.float32)
        part = part.reshape(2, wide, quarter, part.shape[-1])
        p_send[n] = part[1].astype(jnp.bfloat16)
        p_core(n).start()
        p_sum[n] = part[0]

    def p_on(n):
        p_core(n).wait_recv()
        summed = p_sum[n] + p_recv[n].astype(jnp.float32)
        p_sum[n] = summed
        p_send2[n] = summed.astype(jnp.bfloat16)
        each(1, wide, lambda i: p_wide(n, i).start())

    def x_far(k, i):
        return remote(
            x.at[k, 0, a],
            x.at[k, 0, a],
            x_zs.at[k, i],
            x_zr.at[k, a],
            at_a(lax.rem(a + i, far)),
        )

    def x_from(k, source):
        return remote(
            x.at[k, 0, source],
            x.at[k, 0, source],
            x_zs.at[k, 0],
            x_zr.at[k, source],
            beside,
        )

    def x_beside(k, source):
        return remote(
            x.at[k, 0, source],
            x.at[k, 1, source],
            x_ys.at[k, source],
            x_yr.at[k, source],
            beside,
        )

    def x_pass(k):
        def one(i):
            source = lax.rem(a + i, far)
            x_from(k, source).wait_recv()
            x_beside(k, source).start()

        each(1, far, one)

    def inv_far(i):
        return remote(
            inv_buf.at[0, a],
            inv_buf.at[0, a],
            inv_zs.at[i],
            inv_zr.at[a],
            at_a(lax.rem(a + i, far)),
        )

    def inv_from(source):
        return remote(
            inv_buf.at[0, source],
            inv_buf.at[0, source],
            inv_zs.at[0],
            inv_zr.at[source],
            beside,
        )

    def inv_beside(source):
        return remote(
            inv_buf.at[0, source],
            inv_buf.at[1, source],
            inv_ys.at[source],
            inv_yr.at[source],
            beside,
        )

    def inv_pass(i):
        source = lax.rem(a + i, far)
        inv_from(source).wait_recv()
        inv_beside(source).start()

    def p_end(n, square):
        cols = slice(n * width, (n + 1) * width)
        head_sum = p_sum[n, e]
        for i in range(1, wide):
            source = lax.rem(e + i, wide)
            p_from(n, source).wait_recv()
            head_sum = head_sum + p_recv2[n, source].astype(jnp.float32)
        att = (res_buf[:, cols].astype(jnp.float32) + head_sum).astype(jnp.bfloat16)
        att = att.astype(jnp.float32)
        attended[:, cols] = att
        gain = gain_buf[cols].astype(jnp.float32).reshape(1, width)
        x[n, 0, a] = (att * gain).astype(jnp.bfloat16)
        each(1, far, lambda i: x_far(n, i).start())
        x_beside(n, a).start()
        return square + jnp.sum(att * att, axis=-1, keepdims=True)

    for copy in small_copies()[2:]:
        copy.wait()
    square = jnp.zeros((quarter, 1), jnp.float32)
    for step in range(pieces + 7):
        if step < pieces:
            p_step(step)
        if 0 <= step - 3 < pieces:
            p_on(step - 3)
        if 0 <= step - 7 < pieces:
            square = p_end(step - 7, square)
        if step == pieces:
            start_pair(4)
        if step >= pieces + 7 - AHEAD:
            x_pass(step - (pieces + 7 - AHEAD))
    inverse = lax.rsqrt(square / (pieces * width) + 1e-6)
    inv_buf[0, a] = jnp.broadcast_to(inverse, inv_buf.shape[2:])
    each(1, far, lambda i: inv_far(i).start())
    inv_beside(a).start()
    start_pair(5)

    rows = 2 * far * quarter

    def expand(k):
        @pl.when(k + AHEAD < pieces)
        def _():
            x_pass(k + AHEAD)

        @pl.when(k == 2)
        def _():
            each(1, far, inv_pass)

        @pl.when(k + 6 < pieces)
        def _():
            start_pair(k + 6)

        @pl.when((k >= 1) & (k <= slots))
        def _():
            wd_copy(k - 1).start()

        wg_copy(k).wait()
        wu_copy(k).wait()
        each(0, far, lambda source: x_beside(k, source).wait_recv())
        piece = x[k].reshape(rows, width)
        gate_acc[...] += jnp.dot(piece, wg[k], preferred_element_type=jnp.float32)
        up_acc[...] += jnp.dot(piece, wu[k], preferred_element_type=jnp.float32)

    loop(pieces, expand)
    each(0, far, lambda source: inv_beside(source).wait_recv())
    scale = inv_buf[...].reshape(rows, inv_buf.shape[-1])[:, 0:1]
    gate = gate_acc[...] * scale
    up = up_acc[...] * scale
    hidden[...] = (gate / (1.0 + jnp.exp(-gate)) * up).astype(jnp.bfloat16)

    def d_beside(n):
        return remote(d_send.at[n], d_recv.at[n], d_s1.at[n], d_r1.at[n], beside)

    def d_far(n, i):
        other = lax.rem(a + i, far)
        return remote(
            d_send2.at[n, other],
            d_recv2.at[n, a],
            d_s2.at[n, other],
            d_r2.at[n, a],
            at_a(other),
        )

    def d_from(n, source):
        return remote(
            d_send2.at[n, source],
            d_recv2.at[n, source],
            d_s2.at[n, source],
            d_r2.at[n, source],
            at_a(source),
        )

    def d_on(n):
        d_beside(n).wait_recv()
        summed = d_sum[n] + d_recv[n].astype(jnp.float32)
        d_sum[n] = summed
        d_send2[n] = summed.astype(jnp.bfloat16)
        each(1, far, lambda i: d_far(n, i).start())

    def contract(n):
        wd_copy(n).wait()
        part = jnp.dot(hidden[...], wd[n % slots], preferred_element_type=jnp.float32)
        part = part.reshape(2, far, quarter, width)
        d_send[n] = part[1].astype(jnp.bfloat16)
        d_beside(n).start()
        d_sum[n] = part[0]

        @pl.when(n + slots < pieces)
        def _():
            wd_copy(n + slots).start()

        @pl.when(n >= BEHIND)
        def _():
            d_on(n - BEHIND)

    loop(pieces, contract)
    logit = jnp.zeros((quarter, 1), jnp.float32)
    for n in range(pieces):
        cols = slice(n * width, (n + 1) * width)
        gain = gain_buf[cols].astype(jnp.float32).reshape(1, width)
        normed = (attended[:, cols] * inverse * gain).astype(jnp.bfloat16)
        logit_w = logit_buf[cols].astype(jnp.float32).reshape(1, width)
        logit = logit + jnp.sum(
            normed.astype(jnp.float32) * logit_w, axis=-1, keepdims=True
        )
    gate_prob = jax.nn.sigmoid(logit)
    for n in range(max(pieces - BEHIND, 0), pieces):
        d_on(n)
    for n in range(pieces):
        cols = slice(n * width, (n + 1) * width)
        shared = d_sum[n, a]

        def add(i, shared, n=n):
            source = lax.rem(a + i, far)
            d_from(n, source).wait_recv()
            return shared + d_recv2[n, source].astype(jnp.float32)

        if far <= 4:
            for i in range(1, far):
                shared = add(i, shared)
        else:
            shared = lax.fori_loop(1, far, add, shared)
        out[:, cols] = attended[:, cols] + gate_prob * shared

    for w in range(2):
        each(1, far, lambda i, w=w: kv_far(w, i).wait_send())
        each(0, far, lambda source, w=w: kv_beside(w, source).wait_send())
    for n in range(proj_pieces):
        p_core(n).wait_send()
        each(1, wide, lambda i, n=n: p_wide(n, i).wait_send())

    def drain(k):
        each(1, far, lambda i: x_far(k, i).wait_send())
        each(0, far, lambda source: x_beside(k, source).wait_send())
        d_beside(k).wait_send()
        each(1, far, lambda i: d_far(k, i).wait_send())

    loop(pieces, drain)
    each(1, far, lambda i: inv_far(i).wait_send())
    each(0, far, lambda source: inv_beside(source).wait_send())


def per_device(
    queries,
    keys,
    values,
    block_table,
    residual,
    out_weight,
    norm_gain,
    gate_logit_weight,
    gate_weight,
    up_weight,
    down_weight,
):
    tokens = queries.shape[0]
    ctx_count = lax.axis_size("ctx")
    tp_count = lax.axis_size("tp")
    far, wide = ctx_count // 2, tp_count // 2
    quarter, depth = residual.shape
    units = gate_weight.shape[1]
    pieces = depth // WIDTH
    proj_pieces = depth // PROJ
    slots = min(DOWN_SLOTS, pieces)
    rows = ctx_count * quarter
    bf16, f32 = jnp.bfloat16, jnp.float32
    dma = pltpu.SemaphoreType.DMA
    any_space = pl.BlockSpec(memory_space=pl.ANY)
    matmul = rows * depth * units * 3 + tokens * queries.shape[1] * depth
    layer_out = pl.pallas_call(
        functools.partial(kernel, ctx_count, tp_count),
        out_shape=jax.ShapeDtypeStruct((quarter, depth), f32),
        in_specs=[any_space] * 3
        + [pl.BlockSpec(memory_space=pltpu.SMEM)]
        + [any_space] * 7,
        out_specs=pl.BlockSpec(memory_space=pltpu.VMEM),
        scratch_shapes=[
            pltpu.VMEM((2, wide, quarter, queries.shape[1]), bf16),
            pltpu.VMEM((2, 2, far, tokens, HEAD_DIM), bf16),
            pltpu.VMEM((tokens, queries.shape[1]), bf16),
            pltpu.VMEM((quarter, depth), bf16),
            pltpu.VMEM((depth,), bf16),
            pltpu.VMEM((depth,), bf16),
            pltpu.VMEM((proj_pieces, out_weight.shape[0], PROJ), bf16),
            pltpu.VMEM((pieces, WIDTH, units), bf16),
            pltpu.VMEM((pieces, WIDTH, units), bf16),
            pltpu.VMEM((slots, units, WIDTH), bf16),
            pltpu.VMEM((pieces, 2, far, quarter, WIDTH), bf16),
            pltpu.VMEM((rows, units), f32),
            pltpu.VMEM((rows, units), f32),
            pltpu.VMEM((rows, units), bf16),
            pltpu.VMEM((proj_pieces, wide, quarter, PROJ), bf16),
            pltpu.VMEM((proj_pieces, wide, quarter, PROJ), bf16),
            pltpu.VMEM((proj_pieces, wide, quarter, PROJ), bf16),
            pltpu.VMEM((proj_pieces, wide, quarter, PROJ), bf16),
            pltpu.VMEM((proj_pieces, wide, quarter, PROJ), f32),
            pltpu.VMEM((quarter, depth), f32),
            pltpu.VMEM((pieces, far, quarter, WIDTH), bf16),
            pltpu.VMEM((pieces, far, quarter, WIDTH), bf16),
            pltpu.VMEM((pieces, far, quarter, WIDTH), bf16),
            pltpu.VMEM((pieces, far, quarter, WIDTH), bf16),
            pltpu.VMEM((pieces, far, quarter, WIDTH), f32),
            dma((2, wide)),
            dma((5,)),
            dma((proj_pieces,)),
            dma((pieces,)),
            dma((pieces,)),
            dma((pieces,)),
            dma((2, far)),
            dma((2, far)),
            dma((2, far)),
            dma((2, far)),
            dma((pieces, far)),
            dma((pieces, far)),
            dma((pieces, far)),
            dma((pieces, far)),
            dma((proj_pieces,)),
            dma((proj_pieces,)),
            dma((proj_pieces, wide)),
            dma((proj_pieces, wide)),
            dma((pieces,)),
            dma((pieces,)),
            dma((pieces, far)),
            dma((pieces, far)),
            pltpu.VMEM((2, far, quarter, 128), f32),
            dma((far,)),
            dma((far,)),
            dma((far,)),
            dma((far,)),
        ],
        compiler_params=pltpu.CompilerParams(
            collective_id=0,
            has_side_effects=True,
            vmem_limit_bytes=63 * 1024 * 1024,
        ),
        cost_estimate=pl.CostEstimate(
            flops=2 * matmul,
            bytes_accessed=2 * (3 * depth * units + out_weight.size),
            transcendentals=rows * units,
        ),
        name="layer",
    )(
        queries,
        keys,
        values,
        block_table,
        residual,
        out_weight,
        norm_gain,
        gate_logit_weight,
        gate_weight,
        up_weight,
        down_weight,
    )
    return layer_out.astype(bf16)


def solution(mesh):
    return jax.shard_map(
        per_device,
        mesh=mesh,
        in_specs=(
            P("ctx", "tp"),
            P("ctx", "tp"),
            P("ctx", "tp"),
            P(),
            P(("ctx", "tp"), None),
            P("tp", None),
            P(),
            P(),
            P(None, "ctx"),
            P(None, "ctx"),
            P("ctx", None),
        ),
        out_specs=P(("ctx", "tp"), None),
        check_vma=False,
    )
```

```python
import functools

import jax
import jax.numpy as jnp
from jax import lax
from jax.experimental import pallas as pl
from jax.experimental.pallas import tpu as pltpu
from jax.sharding import PartitionSpec as P

HEADS = 28
KV_HEADS = 4
HEAD_DIM = 128
GROUP = HEADS // KV_HEADS
WIDTH = 512
PROJ = WIDTH
TILE = 256
DOWN_SLOTS = 4
AHEAD = 2
BEHIND = 3
MESH = pl.DeviceIdType.MESH


def each(first, last, body):
    if last - first <= 4:
        for index in range(first, last):
            body(index)
    else:
        lax.fori_loop(first, last, lambda i, c: (body(i), c)[1], 0)


def loop(count, body):
    lax.fori_loop(0, count, lambda i, c: (body(i), c)[1], 0)


def kernel(
    ctx_count,
    tp_count,
    queries,
    keys,
    values,
    block_table,
    residual,
    out_weight,
    norm_gain,
    logit_weight,
    gate_weight,
    up_weight,
    down_weight,
    out,
    q_buf,
    kv_buf,
    heads_buf,
    res_buf,
    gain_buf,
    logit_buf,
    wo,
    wg,
    wu,
    wd,
    x,
    gate_acc,
    up_acc,
    hidden,
    p_send,
    p_recv,
    p_send2,
    p_recv2,
    p_sum,
    attended,
    d_send,
    d_recv,
    d_send2,
    d_recv2,
    d_sum,
    sem_q,
    sem_small,
    sem_wo,
    sem_wg,
    sem_wu,
    sem_wd,
    kv_zs,
    kv_zr,
    kv_ys,
    kv_yr,
    x_zs,
    x_zr,
    x_ys,
    x_yr,
    p_s1,
    p_r1,
    p_s2,
    p_r2,
    d_s1,
    d_r1,
    d_s2,
    d_r2,
    inv_buf,
    inv_zs,
    inv_zr,
    inv_ys,
    inv_yr,
):
    far = ctx_count // 2
    wide = tp_count // 2
    me = lax.axis_index("ctx")
    tp = lax.axis_index("tp")
    a, b = me // 2, me % 2
    e, f = tp // 2, tp % 2
    tokens = q_buf.shape[0] * q_buf.shape[1] * q_buf.shape[2]
    quarter = q_buf.shape[2]
    half = tokens // 2
    pieces = x.shape[0]
    proj_pieces = wo.shape[0]
    slots = wd.shape[0]
    width = x.shape[-1]

    def at_a(other):
        return (other * 2 + b, tp)

    beside = (a * 2 + (1 - b), tp)

    def at_e(other):
        return (me, other * 2 + f)

    core = (me, e * 2 + (1 - f))

    def q_copy(rel, i):
        row = pl.multiple_of((i * 2 + (f if rel == 0 else 1 - f)) * quarter, quarter)
        return pltpu.make_async_copy(
            queries.at[pl.ds(row, quarter), :], q_buf.at[rel, i], sem_q.at[rel, i]
        )

    def small_copies():
        return (
            pltpu.make_async_copy(keys, kv_buf.at[0, 0, a], sem_small.at[0]),
            pltpu.make_async_copy(values, kv_buf.at[1, 0, a], sem_small.at[1]),
            pltpu.make_async_copy(residual, res_buf, sem_small.at[2]),
            pltpu.make_async_copy(norm_gain, gain_buf, sem_small.at[3]),
            pltpu.make_async_copy(logit_weight, logit_buf, sem_small.at[4]),
        )

    def wo_copy(n):
        column = pl.multiple_of(n * wo.shape[2], 128)
        return pltpu.make_async_copy(
            out_weight.at[:, pl.ds(column, wo.shape[2])], wo.at[n], sem_wo.at[n]
        )

    def wg_copy(k):
        row = pl.multiple_of(k * width, width)
        return pltpu.make_async_copy(
            gate_weight.at[pl.ds(row, width), :], wg.at[k], sem_wg.at[k]
        )

    def wu_copy(k):
        row = pl.multiple_of(k * width, width)
        return pltpu.make_async_copy(
            up_weight.at[pl.ds(row, width), :], wu.at[k], sem_wu.at[k]
        )

    def wd_copy(n):
        column = pl.multiple_of(n * width, width)
        return pltpu.make_async_copy(
            down_weight.at[:, pl.ds(column, width)], wd.at[n % slots], sem_wd.at[n]
        )

    for copy in small_copies():
        copy.start()
    for rel in range(2):
        for i in range(wide):
            q_copy(rel, i).start()
    for n in range(proj_pieces):
        wo_copy(n).start()

    def start_pair(k):
        wg_copy(k).start()
        wu_copy(k).start()

    loop(pieces, start_pair)
    loop(slots, lambda n: wd_copy(n).start())

    barrier = pltpu.get_barrier_semaphore()

    def greet(device):
        pl.semaphore_signal(barrier, inc=1, device_id=device, device_id_type=MESH)

    greet(beside)
    greet(core)
    each(1, far, lambda i: greet(at_a(lax.rem(a + i, far))))
    each(1, wide, lambda i: greet(at_e(lax.rem(e + i, wide))))
    pl.semaphore_wait(barrier, 2 + far - 1 + wide - 1)

    def remote(src, dst, send, recv, device):
        return pltpu.make_async_remote_copy(
            src_ref=src,
            dst_ref=dst,
            send_sem=send,
            recv_sem=recv,
            device_id=device,
            device_id_type=MESH,
        )

    def kv_far(w, i):
        return remote(
            kv_buf.at[w, 0, a],
            kv_buf.at[w, 0, a],
            kv_zs.at[w, i],
            kv_zr.at[w, a],
            at_a(lax.rem(a + i, far)),
        )

    def kv_from(w, source):
        return remote(
            kv_buf.at[w, 0, source],
            kv_buf.at[w, 0, source],
            kv_zs.at[w, 0],
            kv_zr.at[w, source],
            beside,
        )

    def kv_beside(w, source):
        return remote(
            kv_buf.at[w, 0, source],
            kv_buf.at[w, 1, source],
            kv_ys.at[w, source],
            kv_yr.at[w, source],
            beside,
        )

    for w in range(2):
        small_copies()[w].wait()
        each(1, far, lambda i, w=w: kv_far(w, i).start())
        kv_beside(w, a).start()

    key_count = 2 * far * tokens
    row = lax.broadcasted_iota(jnp.int32, (1, key_count), 1)
    slot = row // tokens
    local = row % tokens

    def place_slot(c, pair):
        owner = (c % far) * 2 + lax.rem(b + c // far, 2)
        return jnp.where(slot == c, block_table[owner], pair)

    pair = lax.fori_loop(
        0, 2 * far, place_slot, jnp.zeros((1, key_count), jnp.int32)
    )
    mirror = 2 * ctx_count - 1
    key_place = jnp.where(
        local < half, pair * half + local, (mirror - pair) * half + local - half
    )
    q_row = lax.broadcasted_iota(jnp.int32, (tokens, 1), 0)
    q_block = q_row // quarter
    q_core = jnp.where(q_block < wide, f, 1 - f)
    q_local = ((q_block % wide) * 2 + q_core) * quarter + q_row % quarter
    own = block_table[me]
    q_place = jnp.where(
        q_local < half, own * half + q_local, (mirror - own) * half + q_local - half
    )
    gate_acc[...] = jnp.zeros_like(gate_acc)
    up_acc[...] = jnp.zeros_like(up_acc)

    def kv_pass(i):
        source = lax.rem(a + i, far)
        for w in range(2):
            kv_from(w, source).wait_recv()
            kv_beside(w, source).start()

    each(1, far, kv_pass)
    for rel in range(2):
        for i in range(wide):
            q_copy(rel, i).wait()

    def kv_arrived(source):
        for w in range(2):
            kv_beside(w, source).wait_recv()

    each(0, far, kv_arrived)

    visible = key_place <= q_place
    all_keys = kv_buf[0].reshape(key_count, HEAD_DIM)
    all_values = kv_buf[1].reshape(key_count, HEAD_DIM)
    for head in range(GROUP):
        lanes = slice(head * HEAD_DIM, (head + 1) * HEAD_DIM)
        q_head = q_buf[:, :, :, lanes].reshape(tokens, HEAD_DIM)
        score = lax.dot_general(
            q_head,
            all_keys,
            (((1,), (1,)), ((), ())),
            preferred_element_type=jnp.float32,
        ) * (HEAD_DIM**-0.5)
        score = jnp.where(visible, score, -1e30)
        top = jnp.max(score, axis=-1, keepdims=True)
        weight = jnp.where(visible, jnp.exp(score - top), 0.0)
        total = jnp.sum(weight, axis=-1, keepdims=True)
        added = jnp.dot(
            weight.astype(jnp.bfloat16), all_values, preferred_element_type=jnp.float32
        )
        heads_buf[:, lanes] = (added / total).astype(jnp.bfloat16)

    def p_core(n):
        return remote(p_send.at[n], p_recv.at[n], p_s1.at[n], p_r1.at[n], core)

    def p_wide(n, i):
        other = lax.rem(e + i, wide)
        return remote(
            p_send2.at[n, other],
            p_recv2.at[n, e],
            p_s2.at[n, other],
            p_r2.at[n, e],
            at_e(other),
        )

    def p_from(n, source):
        return remote(
            p_send2.at[n, source],
            p_recv2.at[n, source],
            p_s2.at[n, source],
            p_r2.at[n, source],
            at_e(source),
        )

    def p_step(n):
        wo_copy(n).wait()
        part = jnp.dot(heads_buf[...], wo[n], preferred_element_type=jnp.float32)
        part = part.reshape(2, wide, quarter, part.shape[-1])
        p_send[n] = part[1].astype(jnp.bfloat16)
        p_core(n).start()
        p_sum[n] = part[0]

    def p_on(n):
        p_core(n).wait_recv()
        summed = p_sum[n] + p_recv[n].astype(jnp.float32)
        p_sum[n] = summed
        p_send2[n] = summed.astype(jnp.bfloat16)
        each(1, wide, lambda i: p_wide(n, i).start())

    def x_far(k, i):
        return remote(
            x.at[k, 0, a],
            x.at[k, 0, a],
            x_zs.at[k, i],
            x_zr.at[k, a],
            at_a(lax.rem(a + i, far)),
        )

    def x_from(k, source):
        return remote(
            x.at[k, 0, source],
            x.at[k, 0, source],
            x_zs.at[k, 0],
            x_zr.at[k, source],
            beside,
        )

    def x_beside(k, source):
        return remote(
            x.at[k, 0, source],
            x.at[k, 1, source],
            x_ys.at[k, source],
            x_yr.at[k, source],
            beside,
        )

    def x_pass(k):
        def one(i):
            source = lax.rem(a + i, far)
            x_from(k, source).wait_recv()
            x_beside(k, source).start()

        each(1, far, one)

    def inv_far(i):
        return remote(
            inv_buf.at[0, a],
            inv_buf.at[0, a],
            inv_zs.at[i],
            inv_zr.at[a],
            at_a(lax.rem(a + i, far)),
        )

    def inv_from(source):
        return remote(
            inv_buf.at[0, source],
            inv_buf.at[0, source],
            inv_zs.at[0],
            inv_zr.at[source],
            beside,
        )

    def inv_beside(source):
        return remote(
            inv_buf.at[0, source],
            inv_buf.at[1, source],
            inv_ys.at[source],
            inv_yr.at[source],
            beside,
        )

    def inv_pass(i):
        source = lax.rem(a + i, far)
        inv_from(source).wait_recv()
        inv_beside(source).start()

    def p_end(n, square):
        cols = slice(n * width, (n + 1) * width)
        head_sum = p_sum[n, e]
        for i in range(1, wide):
            source = lax.rem(e + i, wide)
            p_from(n, source).wait_recv()
            head_sum = head_sum + p_recv2[n, source].astype(jnp.float32)
        att = (res_buf[:, cols].astype(jnp.float32) + head_sum).astype(jnp.bfloat16)
        attended[:, cols] = att
        att = att.astype(jnp.float32)
        gain = gain_buf[cols].astype(jnp.float32).reshape(1, width)
        x[n, 0, a] = (att * gain).astype(jnp.bfloat16)
        each(1, far, lambda i: x_far(n, i).start())
        x_beside(n, a).start()
        return square + jnp.sum(att * att, axis=-1, keepdims=True)

    for copy in small_copies()[2:]:
        copy.wait()
    square = jnp.zeros((quarter, 1), jnp.float32)
    for step in range(pieces + 7):
        if step < pieces:
            p_step(step)
        if 0 <= step - 3 < pieces:
            p_on(step - 3)
        if 0 <= step - 7 < pieces:
            square = p_end(step - 7, square)
        if step >= pieces + 7 - AHEAD:
            x_pass(step - (pieces + 7 - AHEAD))
    inverse = lax.rsqrt(square / (pieces * width) + 1e-6)
    inv_buf[0, a] = jnp.broadcast_to(inverse, inv_buf.shape[2:])
    each(1, far, lambda i: inv_far(i).start())
    inv_beside(a).start()

    rows = 2 * far * quarter
    units = hidden.shape[1]
    size = TILE if units % TILE == 0 else units
    tiles = [slice(first, first + size) for first in range(0, units, size)]

    def expand(k):
        @pl.when(k + AHEAD < pieces)
        def _():
            x_pass(k + AHEAD)

        @pl.when(k == 2)
        def _():
            each(1, far, inv_pass)

        wg_copy(k).wait()
        wu_copy(k).wait()
        each(0, far, lambda source: x_beside(k, source).wait_recv())
        piece = x[k].reshape(rows, width)
        for tile in tiles:
            gate_acc[:, tile] += jnp.dot(
                piece, wg[k, :, tile], preferred_element_type=jnp.float32
            )
            up_acc[:, tile] += jnp.dot(
                piece, wu[k, :, tile], preferred_element_type=jnp.float32
            )

    loop(pieces, expand)
    each(0, far, lambda source: inv_beside(source).wait_recv())
    scale = inv_buf[...].reshape(rows, inv_buf.shape[-1])[:, 0:1]
    for tile in tiles:
        gate = gate_acc[:, tile] * scale
        up = up_acc[:, tile] * scale
        hidden[:, tile] = (gate / (1.0 + jnp.exp(-gate)) * up).astype(jnp.bfloat16)

    def d_beside(n):
        return remote(d_send.at[n], d_recv.at[n], d_s1.at[n], d_r1.at[n], beside)

    def d_far(n, i):
        other = lax.rem(a + i, far)
        return remote(
            d_send2.at[n, other],
            d_recv2.at[n, a],
            d_s2.at[n, other],
            d_r2.at[n, a],
            at_a(other),
        )

    def d_from(n, source):
        return remote(
            d_send2.at[n, source],
            d_recv2.at[n, source],
            d_s2.at[n, source],
            d_r2.at[n, source],
            at_a(source),
        )

    def d_on(n):
        d_beside(n).wait_recv()
        summed = d_sum[n] + d_recv[n].astype(jnp.float32)
        d_sum[n] = summed
        d_send2[n] = summed.astype(jnp.bfloat16)
        each(1, far, lambda i: d_far(n, i).start())

    def contract(n):
        wd_copy(n).wait()
        part = jnp.dot(hidden[...], wd[n % slots], preferred_element_type=jnp.float32)
        part = part.reshape(2, far, quarter, width)
        d_send[n] = part[1].astype(jnp.bfloat16)
        d_beside(n).start()
        d_sum[n] = part[0]

        @pl.when(n + slots < pieces)
        def _():
            wd_copy(n + slots).start()

        @pl.when(n >= BEHIND)
        def _():
            d_on(n - BEHIND)

    loop(pieces, contract)
    logit = jnp.zeros((quarter, 1), jnp.float32)
    for n in range(pieces):
        cols = slice(n * width, (n + 1) * width)
        gain = gain_buf[cols].astype(jnp.float32).reshape(1, width)
        normed = (attended[:, cols].astype(jnp.float32) * inverse * gain).astype(jnp.bfloat16)
        logit_w = logit_buf[cols].astype(jnp.float32).reshape(1, width)
        logit = logit + jnp.sum(
            normed.astype(jnp.float32) * logit_w, axis=-1, keepdims=True
        )
    gate_prob = jax.nn.sigmoid(logit)
    for n in range(max(pieces - BEHIND, 0), pieces):
        d_on(n)
    for n in range(pieces):
        cols = slice(n * width, (n + 1) * width)
        shared = d_sum[n, a]

        def add(i, shared, n=n):
            source = lax.rem(a + i, far)
            d_from(n, source).wait_recv()
            return shared + d_recv2[n, source].astype(jnp.float32)

        if far <= 4:
            for i in range(1, far):
                shared = add(i, shared)
        else:
            shared = lax.fori_loop(1, far, add, shared)
        out[:, cols] = attended[:, cols].astype(jnp.float32) + gate_prob * shared

    for w in range(2):
        each(1, far, lambda i, w=w: kv_far(w, i).wait_send())
        each(0, far, lambda source, w=w: kv_beside(w, source).wait_send())
    for n in range(proj_pieces):
        p_core(n).wait_send()
        each(1, wide, lambda i, n=n: p_wide(n, i).wait_send())

    def drain(k):
        each(1, far, lambda i: x_far(k, i).wait_send())
        each(0, far, lambda source: x_beside(k, source).wait_send())
        d_beside(k).wait_send()
        each(1, far, lambda i: d_far(k, i).wait_send())

    loop(pieces, drain)
    each(1, far, lambda i: inv_far(i).wait_send())
    each(0, far, lambda source: inv_beside(source).wait_send())


def per_device(
    queries,
    keys,
    values,
    block_table,
    residual,
    out_weight,
    norm_gain,
    gate_logit_weight,
    gate_weight,
    up_weight,
    down_weight,
):
    tokens = queries.shape[0]
    ctx_count = lax.axis_size("ctx")
    tp_count = lax.axis_size("tp")
    far, wide = ctx_count // 2, tp_count // 2
    quarter, depth = residual.shape
    units = gate_weight.shape[1]
    pieces = depth // WIDTH
    proj_pieces = depth // PROJ
    slots = min(DOWN_SLOTS, pieces)
    rows = ctx_count * quarter
    bf16, f32 = jnp.bfloat16, jnp.float32
    dma = pltpu.SemaphoreType.DMA
    any_space = pl.BlockSpec(memory_space=pl.ANY)
    matmul = rows * depth * units * 3 + tokens * queries.shape[1] * depth
    layer_out = pl.pallas_call(
        functools.partial(kernel, ctx_count, tp_count),
        out_shape=jax.ShapeDtypeStruct((quarter, depth), f32),
        in_specs=[any_space] * 3
        + [pl.BlockSpec(memory_space=pltpu.SMEM)]
        + [any_space] * 7,
        out_specs=pl.BlockSpec(memory_space=pltpu.VMEM),
        scratch_shapes=[
            pltpu.VMEM((2, wide, quarter, queries.shape[1]), bf16),
            pltpu.VMEM((2, 2, far, tokens, HEAD_DIM), bf16),
            pltpu.VMEM((tokens, queries.shape[1]), bf16),
            pltpu.VMEM((quarter, depth), bf16),
            pltpu.VMEM((depth,), bf16),
            pltpu.VMEM((depth,), bf16),
            pltpu.VMEM((proj_pieces, out_weight.shape[0], PROJ), bf16),
            pltpu.VMEM((pieces, WIDTH, units), bf16),
            pltpu.VMEM((pieces, WIDTH, units), bf16),
            pltpu.VMEM((slots, units, WIDTH), bf16),
            pltpu.VMEM((pieces, 2, far, quarter, WIDTH), bf16),
            pltpu.VMEM((rows, units), f32),
            pltpu.VMEM((rows, units), f32),
            pltpu.VMEM((rows, units), bf16),
            pltpu.VMEM((proj_pieces, wide, quarter, PROJ), bf16),
            pltpu.VMEM((proj_pieces, wide, quarter, PROJ), bf16),
            pltpu.VMEM((proj_pieces, wide, quarter, PROJ), bf16),
            pltpu.VMEM((proj_pieces, wide, quarter, PROJ), bf16),
            pltpu.VMEM((proj_pieces, wide, quarter, PROJ), f32),
            pltpu.VMEM((quarter, depth), bf16),
            pltpu.VMEM((pieces, far, quarter, WIDTH), bf16),
            pltpu.VMEM((pieces, far, quarter, WIDTH), bf16),
            pltpu.VMEM((pieces, far, quarter, WIDTH), bf16),
            pltpu.VMEM((pieces, far, quarter, WIDTH), bf16),
            pltpu.VMEM((pieces, far, quarter, WIDTH), f32),
            dma((2, wide)),
            dma((5,)),
            dma((proj_pieces,)),
            dma((pieces,)),
            dma((pieces,)),
            dma((pieces,)),
            dma((2, far)),
            dma((2, far)),
            dma((2, far)),
            dma((2, far)),
            dma((pieces, far)),
            dma((pieces, far)),
            dma((pieces, far)),
            dma((pieces, far)),
            dma((proj_pieces,)),
            dma((proj_pieces,)),
            dma((proj_pieces, wide)),
            dma((proj_pieces, wide)),
            dma((pieces,)),
            dma((pieces,)),
            dma((pieces, far)),
            dma((pieces, far)),
            pltpu.VMEM((2, far, quarter, 128), f32),
            dma((far,)),
            dma((far,)),
            dma((far,)),
            dma((far,)),
        ],
        compiler_params=pltpu.CompilerParams(
            collective_id=0,
            has_side_effects=True,
            vmem_limit_bytes=63 * 1024 * 1024,
        ),
        cost_estimate=pl.CostEstimate(
            flops=2 * matmul,
            bytes_accessed=2 * (3 * depth * units + out_weight.size),
            transcendentals=rows * units,
        ),
        name="layer",
    )(
        queries,
        keys,
        values,
        block_table,
        residual,
        out_weight,
        norm_gain,
        gate_logit_weight,
        gate_weight,
        up_weight,
        down_weight,
    )
    return layer_out.astype(bf16)


def solution(mesh):
    return jax.shard_map(
        per_device,
        mesh=mesh,
        in_specs=(
            P("ctx", "tp"),
            P("ctx", "tp"),
            P("ctx", "tp"),
            P(),
            P(("ctx", "tp"), None),
            P("tp", None),
            P(),
            P(),
            P(None, "ctx"),
            P(None, "ctx"),
            P("ctx", None),
        ),
        out_specs=P(("ctx", "tp"), None),
        check_vma=False,
    )
```
